32 devices in a mesh: dom: 4 (over x, core), row: 8 (over z, y).
Axes of the slice: x: 2, y: 2, z: 4, core: 2. Of those that a mesh axis runs over, the one named last changes fastest.
Arguments:
- entity_table: float32 [4, 2048, 400], P('dom', 'row'), may hold values from -1.5 to 1.5
- adagrad_state: float32 [4, 2048], P('dom', 'row'), may hold values from 0.05 to 0.5
- relations: bfloat16 [16, 400], replicated, may hold values from -4 to 4
- sources: int32 [2, 4, 3072], P(None, 'dom', 'row'), may hold values from 0 to 2047, as said below
- targets: int32 [2, 4, 3072], P(None, 'dom', 'row'), may hold values from 0 to 2047, as said below
- relation_ids: int32 [2, 4, 3072], P(None, 'dom', 'row'), may hold values from 0 to 15
- edge_counts: int32 [2, 4, 8], P(None, 'dom', 'row'), may hold values from 96 to 384, as said below
Outputs:
- new_table: float32 [4, 2048, 400], P('dom', 'row')
- new_state: float32 [4, 2048], P('dom', 'row')
The draws below stay inside these ranges and needn't reach their ends.
Inputs may be any that keep to these rules, and one draw needn't show every extreme that they name: `edge_counts`: in every round some aligned block is full, holding 384 live edges; the live edges of a block are its first slots. `sources`: in every round and bucket, the 384 slots of one aligned block name rows of any one run of 256 rows (rows with the same row div 256) at most 96 times, and in every block some run exactly 96 times. `targets`: in every round and bucket, the 384 slots of one aligned block name rows of any one run of 256 rows (rows with the same row div 256) at most 96 times, and in every block some run exactly 96 times.
All inputs are finite; a program needn't handle non-finite values.
Results may differ from the reference program's by a relative error of at most 0.0019.
Values may be sent and summed in bfloat16 or wider, within the bound.
No kernel may reach another device: no remote copies, remote signals or barrier semaphores. Data moves between devices by JAX's collectives and lax.ppermute only.
A program may use at most 64 MiB of HBM per device.

```python
import math
import jax
import jax.numpy as jnp
from jax import lax

WIDTH = 400
NREL = 16
ROWS_DEV = 256
E_DEV = 384
GROUP = 384
ROUNDS = 2
PARTS_SIZE = 4
ROWS = 2048
EDGES = 3072
N_ROW = 8


def holder_rows(key):
    blocks = ROUNDS * PARTS_SIZE * N_ROW
    block_keys = jax.random.split(key, blocks)
    share = E_DEV // N_ROW

    def one_block(block_key):
        order_key, moved_key, shuffle_key, offset_key = jax.random.split(block_key, 4)
        order = jax.random.permutation(order_key, N_ROW)
        moved = jax.random.randint(moved_key, (N_ROW // 2,), 0, share + 1)
        moved = moved.at[0].set(share)
        counts = jnp.zeros((N_ROW,), jnp.int32)
        counts = counts.at[order[0::2]].set(share + moved)
        counts = counts.at[order[1::2]].set(share - moved)
        ends = jnp.cumsum(counts)
        slots = jnp.arange(E_DEV)
        holder = jnp.sum((slots[:, None] >= ends[None, :]).astype(jnp.int32), axis=-1)
        holder = jax.random.permutation(shuffle_key, holder)
        offset = jax.random.randint(offset_key, (E_DEV,), 0, ROWS_DEV)
        return holder * ROWS_DEV + offset
    picked = jax.vmap(one_block)(block_keys)
    return picked.reshape(ROUNDS, PARTS_SIZE, N_ROW * E_DEV).astype(jnp.int32)


def draw_sources(key, part):
    key = jax.random.fold_in(key, 23)
    return holder_rows(key)


def draw_targets(key, part):
    key = jax.random.fold_in(key, 37)
    return holder_rows(key)


def draw_edge_counts(key, part):
    key = jax.random.fold_in(key, 11)
    first_key, second_key = jax.random.split(key)
    blocks = PARTS_SIZE * N_ROW
    base = jax.random.randint(first_key, (ROUNDS, blocks), E_DEV // 4, E_DEV + 1)
    chosen = jax.random.randint(second_key, (ROUNDS, 1), 0, blocks)
    filled = jnp.where(jnp.arange(blocks)[None, :] == chosen, E_DEV, base)
    return filled.reshape(ROUNDS, PARTS_SIZE, N_ROW).astype(jnp.int32)


def set_ends(drawn, rng, smallest, largest):
    shape = drawn.shape
    place = [jax.random.randint(jax.random.fold_in(rng, axis), (), 0, shape[axis]) for axis in range(len(shape))]
    drawn = drawn.at[tuple(place)].set(smallest)
    longest = shape.index(max(shape))
    place[longest] = (place[longest] + 1) % shape[longest]
    return drawn.at[tuple(place)].set(largest)


def levels(own_key, extent, shards, low, top_value):
    def one(axis_at, shards_of):
        draws = jax.random.uniform(jax.random.fold_in(jax.random.fold_in(own_key, 6), axis_at), (shards_of,), jnp.float32, low / len(shards), top_value / len(shards))
        return jnp.repeat(jnp.exp(draws), extent[axis_at] // shards_of).reshape((-1,) + (1,) * (len(extent) - axis_at - 1))

    loudness = one(*shards[0])
    for cut in shards[1:]:
        loudness = loudness * one(*cut)
    return loudness


def bell_draw(stream_key, extent, spread, most, shards=(), kind=jnp.bfloat16):
    loudness = levels(stream_key, extent, shards, -0.22, 0.18) if shards else 1.0
    values = jax.random.normal(stream_key, extent, jnp.float32) * spread * loudness
    return jnp.minimum(jnp.maximum(values, -most), most).astype(kind)


def setup_inputs(seed: int = 0) -> dict:
    arg_keys = jax.random.split(jax.random.key(seed), 8)
    return {
        "entity_table": bell_draw(arg_keys[0], (PARTS_SIZE, ROWS, WIDTH), 0.25, 1.5, ((0, 4), (1, 8)), jnp.float32),
        "adagrad_state": jnp.clip(jnp.exp(math.log(0.5) - 2.3025851 * jax.random.uniform(arg_keys[1], (PARTS_SIZE, ROWS), jnp.float32) ** levels(arg_keys[1], (PARTS_SIZE, ROWS), ((0, 4), (1, 8)), -0.2, 0.2)), 0.05, 0.5),
        "relations": bell_draw(arg_keys[2], (NREL, WIDTH), 0.7, 4.0),
        "sources": draw_sources(jax.random.fold_in(arg_keys[7], 71), 0),
        "targets": draw_targets(jax.random.fold_in(arg_keys[7], 71), 0),
        "relation_ids": set_ends(jax.random.randint(arg_keys[5], (ROUNDS, PARTS_SIZE, EDGES), 0, NREL), jax.random.fold_in(arg_keys[5], 1), 0, NREL - 1).astype(jnp.int32),
        "edge_counts": draw_edge_counts(jax.random.fold_in(arg_keys[7], 71), 0),
    }


learn_rate = 0.1

def edge_grads(src_rows, dst_rows, rel_rows, live_mask):
    half_width = src_rows.shape[-1] // 2
    source = src_rows.astype(jnp.float32)
    relate = rel_rows.astype(jnp.float32)
    src_real = source[..., :half_width]
    src_imag = source[..., half_width:]
    rel_real = relate[..., :half_width]
    rel_imag = relate[..., half_width:]
    queries = jnp.concatenate([src_real * rel_real - src_imag * rel_imag, src_real * rel_imag + src_imag * rel_real], -1).astype(jnp.bfloat16)
    targets_f = dst_rows.astype(jnp.float32)
    queries_f = queries.astype(jnp.float32)
    scores = jnp.einsum('bik,bjk->bij', queries_f, targets_f)
    block_size = scores.shape[-1]
    diagonal = jnp.arange(block_size)[:, None] == jnp.arange(block_size)[None, :]
    pair_mask = live_mask[:, :, None] * live_mask[:, None, :]
    weights = (jnp.where(diagonal, -jax.nn.sigmoid(-scores), jax.nn.sigmoid(scores) / block_size) * pair_mask).astype(jnp.bfloat16)
    weights_f = weights.astype(jnp.float32)
    query_grad = jnp.einsum('bij,bjk->bik', weights_f, targets_f)
    dst_grad = jnp.einsum('bij,bik->bjk', weights_f, queries_f)
    grad_real = query_grad[..., :half_width]
    grad_imag = query_grad[..., half_width:]
    src_grad = jnp.concatenate([grad_real * rel_real + grad_imag * rel_imag, grad_imag * rel_real - grad_real * rel_imag], -1)
    return (src_grad.astype(jnp.bfloat16), dst_grad.astype(jnp.bfloat16))

def reference(entity_table, adagrad_state, relations, sources, targets, relation_ids, edge_counts):
    entity = entity_table
    adagrad = adagrad_state
    slot_ids = jnp.arange(EDGES).astype(jnp.int32)
    for round_index in range(ROUNDS):
        shift_by = round_index + 1
        table_b = entity.astype(jnp.bfloat16)
        rhs_tables = jnp.roll(table_b, shift_by, axis=0)
        block_of = (slot_ids // E_DEV).astype(jnp.int32)
        live_all = ((slot_ids % E_DEV)[None, :] < edge_counts[round_index][:, block_of]).astype(jnp.float32)

        def one_bucket(items):
            lhs_rows, rhs_rows, src_ids, dst_ids, rel_ids, live_row = items
            src_grad, dst_grad = edge_grads(lhs_rows[src_ids].reshape(-1, GROUP, WIDTH), rhs_rows[dst_ids].reshape(-1, GROUP, WIDTH), relations[rel_ids].reshape(-1, GROUP, WIDTH), live_row.reshape(-1, GROUP))
            lhs_sum = jax.ops.segment_sum(src_grad.reshape(-1, WIDTH).astype(jnp.float32), src_ids, num_segments=ROWS)
            rhs_sum = jax.ops.segment_sum(dst_grad.reshape(-1, WIDTH).astype(jnp.float32), dst_ids, num_segments=ROWS)
            return (lhs_sum, rhs_sum)
        lhs_sums, rhs_sums = lax.map(one_bucket, (table_b, rhs_tables, sources[round_index], targets[round_index], relation_ids[round_index], live_all))
        gradient = lhs_sums + jnp.roll(rhs_sums, -shift_by, axis=0)
        adagrad = adagrad + lax.optimization_barrier(jnp.mean(gradient * gradient, axis=-1))
        entity = entity - learn_rate * gradient / jnp.sqrt(adagrad)[..., None]
    return (entity, adagrad)
```

```python
import jax
import jax.numpy as jnp
from jax import lax
from jax.experimental import pallas as pl
from jax.experimental.pallas import tpu as pltpu
from jax.sharding import PartitionSpec as P

GROUP = 384
ROUNDS = 2
LANES = 128

learn_rate = 0.1

F32 = jnp.float32
BF16 = jnp.bfloat16
VMEM = pl.BlockSpec(memory_space=pltpu.VMEM)
SMEM = pl.BlockSpec(memory_space=pltpu.SMEM)
PARAMS = pltpu.CompilerParams(vmem_limit_bytes=48 * 1024 * 1024)


def place(x, core, z, y):
    return (x * 2 + core) * 8 + z * 2 + y


PLACES = [(x, c, z, y) for x in range(2) for c in range(2) for z in range(4) for y in range(2)]


def route(target):
    return [(place(*at), place(*target(*at))) for at in PLACES]


def far_z(x, z, y):
    swap = (0, 1, 1, 0)[z] ^ y
    return z ^ ((0, 3), (1, 2))[x][swap]


FIRST = [
    route(lambda x, c, z, y: (x, c, z ^ 1, y) if c == 0 else (x, c, z, y ^ 1)),
    route(lambda x, c, z, y: (x, c, z ^ 2, y) if c == 0 else (x ^ 1, c, z, y)),
    route(lambda x, c, z, y: (x, c, z ^ 3, y) if c == 0 else (x ^ 1, c, z, y ^ 1)),
]
SWAP_CORE = route(lambda x, c, z, y: (x, c ^ 1, z, y))
SWAP_X = route(lambda x, c, z, y: (x ^ 1, c, z, y))
SWAP_Y = route(lambda x, c, z, y: (x, c, z, y ^ 1))
ALONG_Z = [route(lambda x, c, z, y, k=k: (x, c, z ^ k, y)) for k in (1, 2, 3)]
SECOND = [
    SWAP_Y,
    [(place(x ^ 1, c, far_z(x, z, y), y), place(x, c, z, y)) for x, c, z, y in PLACES],
    [(place(x ^ 1, c, far_z(x, z, y), y ^ 1), place(x, c, z, y)) for x, c, z, y in PLACES],
]


def move(value, pairs):
    return lax.ppermute(value, ("dom", "row"), pairs)


def back(pairs):
    return [(target, source) for source, target in pairs]


def plans():
    first, second = [], []
    for x, c, z, y in PLACES:
        line = [(z ^ k) * 2 + y for k in range(4)]
        pair = [z * 2 + y, z * 2 + (y ^ 1)]
        if c == 0:
            entries = [
                (0, line[0], 0), (1, line[1], 1), (6, pair[0], 6), (7, pair[1], 7),
                (2, line[2], 2), (3, line[3], 3), (6, pair[0], 6), (7, pair[1], 7),
            ]
        else:
            entries = [
                (0, pair[0], 0), (1, pair[1], 1), (4, line[0], 4), (5, line[1], 5),
                (0, pair[0], 0), (1, pair[1], 1), (6, line[2], 6), (7, line[3], 7),
            ]
        first.append(entries)
        far = far_z(x, z, y) * 2
        far = [far + y, far + (y ^ 1)]
        second.append([
            (0, pair[0], 0), (1, pair[1], 1), (2, far[0], 2), (3, far[1], 3),
            (2, far[0], 2), (3, far[1], 3), (0, pair[0], 0), (1, pair[1], 1),
        ])
    return jnp.array([first, second], jnp.int32)


def halves(width):
    half = width // 2
    return half, -(-half // 16) * 16


def table_kernel(entity_ref, master_ref, wire_ref):
    rows, width = entity_ref.shape
    half, padded = halves(width)
    full = -(-width // LANES) * LANES
    turned = jnp.pad(entity_ref[...], ((0, 0), (0, full - width))).T
    blank = jnp.zeros((padded - half, rows), F32)
    out = jnp.concatenate([turned[:half], blank, turned[half:width], blank], 0)
    master_ref[...] = out
    wire_ref[...] = out.astype(BF16)


def turn_table(entity):
    rows, width = entity.shape
    padded = 2 * halves(width)[1]
    return pl.pallas_call(
        table_kernel,
        out_shape=(
            jax.ShapeDtypeStruct((padded, rows), F32),
            jax.ShapeDtypeStruct((padded, rows), BF16),
        ),
        in_specs=[VMEM],
        out_specs=(VMEM, VMEM),
        compiler_params=PARAMS,
        name="turn_table",
    )(entity)


def lists_kernel(rows_per, holders, count_ref, source_ref, target_ref, relation_ref, out_ref):
    slots = source_ref.shape[-1]
    total = holders * LANES
    lower = lax.broadcasted_iota(jnp.int32, (slots, slots), 0)
    upper = lax.broadcasted_iota(jnp.int32, (slots, slots), 1)
    before = (lower <= upper).astype(BF16)
    edge = lax.broadcasted_iota(jnp.int32, (1, slots), 1)
    holder_ids = lax.broadcasted_iota(jnp.int32, (holders, slots), 0)
    slot_ids = lax.broadcasted_iota(jnp.int32, (total, slots), 0)
    for round_index in range(ROUNDS):
        live = edge < count_ref[round_index]
        relation = relation_ref[round_index]
        found = []
        for ids_ref in (source_ref, target_ref):
            ids = ids_ref[round_index]
            holder = ids // rows_per
            local = ids - holder * rows_per
            mine = jnp.logical_and(holder_ids == holder, live)
            running = jnp.dot(mine.astype(BF16), before, preferred_element_type=F32)
            rank = jnp.sum(jnp.where(mine, running, 0.0), axis=0, keepdims=True).astype(jnp.int32) - 1
            slot = jnp.where(live, holder * LANES + rank, -1)
            pick = (slot_ids == slot).astype(F32).astype(BF16)
            values = jnp.concatenate(
                [local - 128, relation, edge // 16, edge % 16, jnp.ones_like(edge)]
                + [jnp.zeros_like(edge)] * 3,
                0,
            ).astype(F32).astype(BF16)
            rows = lax.dot_general(
                values, pick, (((1,), (1,)), ((), ())), preferred_element_type=F32
            ).astype(jnp.int32)
            there = rows[4:5] > 0
            ids_row = jnp.where(there, rows[0:1] + 128, 65535)
            edge_row = jnp.where(there, rows[2:3] * 16 + rows[3:4], 511)
            found.append((ids_row, edge_row, rows[1:2]))
        (source_ids, source_edge, relation_row), (target_ids, target_edge, _) = found
        packed = (
            jnp.bitwise_or(source_ids, jnp.left_shift(source_edge, 16)),
            relation_row,
            jnp.bitwise_or(target_ids, jnp.left_shift(target_edge, 16)),
        )
        for kind in range(3):
            for holder in range(holders):
                out_ref[round_index, kind, holder : holder + 1, :] = packed[kind][
                    :, holder * LANES : (holder + 1) * LANES
                ]


def make_lists(sources, targets, relation_ids, edge_counts, rows_per, holders):
    def kernel(*refs):
        lists_kernel(rows_per, holders, *refs)

    return pl.pallas_call(
        kernel,
        out_shape=jax.ShapeDtypeStruct((ROUNDS, 3, holders, LANES), jnp.int32),
        in_specs=[SMEM, VMEM, VMEM, VMEM],
        out_specs=VMEM,
        compiler_params=PARAMS,
        name="make_lists",
    )(edge_counts.reshape(ROUNDS), sources, targets, relation_ids)


def tiles_kernel(
    plan_ref, one_ref, two_ref, relations_ref, near_ref, far_ref, local_ref, cross_ref, tables, sums
):
    blocks = one_ref.shape[0]
    padded = near_ref.shape[1]
    rows = near_ref.shape[2]
    half = padded // 2
    relation_total = relations_ref.shape[1]
    for entry in range(8):
        at = plan_ref[entry, 0]
        spot = jnp.bitwise_and(at, 3)
        tables[entry] = jnp.where(at < 4, near_ref[spot], far_ref[spot])
    sums[...] = jnp.zeros_like(sums)
    row_ids = lax.broadcasted_iota(jnp.int32, (rows, 2 * LANES), 0)
    relation_slots = lax.broadcasted_iota(jnp.int32, (relation_total, 2 * LANES), 0)
    relations = relations_ref[...]

    def step(pair, carry):
        for task, lists in ((0, one_ref), (1, two_ref)):
            picks, gathered, edges, kinds = [], [], [], []
            for side in range(2):
                for k in range(2):
                    entry = task * 4 + side * 2 + k
                    holder = plan_ref[entry, 1]
                    packed = [
                        lists[2 * pair + j, 2 * side, pl.ds(holder, 1), :] for j in range(2)
                    ]
                    ids = jnp.concatenate([jnp.bitwise_and(v, 65535) for v in packed], 1)
                    pick = (row_ids == ids).astype(F32).astype(BF16)
                    picks.append(pick)
                    edges.append([jnp.right_shift(v, 16) for v in packed])
                    gathered.append(
                        jnp.dot(tables[entry], pick, preferred_element_type=F32).astype(BF16)
                    )
                    if side == 0:
                        kinds.append(
                            [lists[2 * pair + j, 1, pl.ds(holder, 1), :] for j in range(2)]
                        )
            source_grads, target_grads = [], []
            for j in range(2):
                cut = slice(j * LANES, (j + 1) * LANES)
                source = jnp.concatenate([gathered[0][:, cut], gathered[1][:, cut]], 1)
                target = jnp.concatenate([gathered[2][:, cut], gathered[3][:, cut]], 1)
                kind = jnp.concatenate([kinds[0][j], kinds[1][j]], 1)
                relate = jnp.dot(
                    relations,
                    (relation_slots == kind).astype(F32).astype(BF16),
                    preferred_element_type=F32,
                )
                relate_re, relate_im = relate[:half], relate[half:]
                source_re, source_im = source[:half].astype(F32), source[half:].astype(F32)
                queries = jnp.concatenate(
                    [
                        source_re * relate_re - source_im * relate_im,
                        source_re * relate_im + source_im * relate_re,
                    ],
                    0,
                ).astype(BF16)
                scores = lax.dot_general(
                    queries, target, (((0,), (0,)), ((), ())), preferred_element_type=F32
                )
                edge_row = jnp.concatenate([edges[2][j], edges[3][j]], 1)
                edge_col = jnp.concatenate([edges[0][j], edges[1][j]], 1).astype(F32)
                edge_col = jnp.broadcast_to(edge_col, (8, 2 * LANES)).T[:, :1].astype(jnp.int32)
                bent = 0.5 * jnp.tanh(0.5 * scores)
                weights = jnp.where(
                    edge_col == edge_row, bent - 0.5, (bent + 0.5) * (1.0 / GROUP)
                ).astype(BF16)
                query_grad = lax.dot_general(
                    target, weights, (((1,), (1,)), ((), ())), preferred_element_type=F32
                )
                target_grads.append(
                    jnp.dot(queries, weights, preferred_element_type=F32).astype(BF16)
                )
                grad_re, grad_im = query_grad[:half], query_grad[half:]
                source_grads.append(
                    jnp.concatenate(
                        [
                            grad_re * relate_re + grad_im * relate_im,
                            grad_im * relate_re - grad_re * relate_im,
                        ],
                        0,
                    ).astype(BF16)
                )
            for side, grads in ((0, source_grads), (1, target_grads)):
                for k in range(2):
                    cut = slice(k * LANES, (k + 1) * LANES)
                    part = jnp.concatenate([grads[0][:, cut], grads[1][:, cut]], 1)
                    spot = plan_ref[task * 4 + side * 2 + k, 2]
                    sums[spot] += lax.dot_general(
                        part,
                        picks[side * 2 + k],
                        (((1,), (1,)), ((), ())),
                        preferred_element_type=F32,
                    )
        return carry

    lax.fori_loop(0, blocks // 2, step, 0)
    local_ref[...] = sums[0:4]
    cross_ref[...] = sums[4:8].astype(BF16)


def tiles(plan, one, two, relations, near, far):
    padded, rows = near.shape[1:]
    return pl.pallas_call(
        tiles_kernel,
        out_shape=(
            jax.ShapeDtypeStruct((4, padded, rows), F32),
            jax.ShapeDtypeStruct((4, padded, rows), BF16),
        ),
        in_specs=[SMEM] + [VMEM] * 5,
        out_specs=(VMEM, VMEM),
        scratch_shapes=[pltpu.VMEM((8, padded, rows), BF16), pltpu.VMEM((8, padded, rows), F32)],
        compiler_params=PARAMS,
        name="tiles",
    )(plan, one, two, relations, near, far)


def update_kernel(width, last, master_ref, state_ref, own_ref, a_ref, b_ref, c_ref, *outs):
    half, padded = halves(width)
    gradient = (own_ref[...] + a_ref[...].astype(F32)) + (
        b_ref[...].astype(F32) + c_ref[...].astype(F32)
    )
    state = state_ref[...] + jnp.sum(gradient * gradient, axis=0, keepdims=True) / width
    master = master_ref[...] - learn_rate * gradient / jnp.sqrt(state)
    outs[1][...] = state
    if not last:
        outs[0][...] = master
        outs[2][...] = master.astype(BF16)
        return
    full = -(-width // LANES) * LANES
    rows = master.shape[1]
    joined = jnp.concatenate(
        [master[:half], master[padded : padded + half], jnp.zeros((full - width, rows), F32)], 0
    )
    outs[0][...] = joined.T[:, :width]


def update(master, state, own, a, b, c, width, last):
    padded, rows = master.shape

    def kernel(*refs):
        update_kernel(width, last, *refs)

    shapes = [
        jax.ShapeDtypeStruct((rows, width) if last else (padded, rows), F32),
        jax.ShapeDtypeStruct((1, rows), F32),
    ]
    if not last:
        shapes.append(jax.ShapeDtypeStruct((padded, rows), BF16))
    return pl.pallas_call(
        kernel,
        out_shape=tuple(shapes),
        in_specs=[VMEM] * 6,
        out_specs=(VMEM,) * len(shapes),
        compiler_params=PARAMS,
        name="update",
    )(master, state, own, a, b, c)


def tile_body(entity_table, adagrad_state, relations, sources, targets, relation_ids, edge_counts):
    rows, width = entity_table.shape[1:]
    half, padded = halves(width)
    holders = lax.axis_size("row")
    me = lax.axis_index("dom") * holders + lax.axis_index("row")
    plan = lax.dynamic_index_in_dim(plans(), me, 1, keepdims=False)
    master, wire = turn_table(entity_table[0])
    state = adagrad_state
    relate = jnp.pad(
        relations.T.reshape(2, half, -1), ((0, 0), (0, padded - half), (0, 0))
    ).reshape(2 * padded, -1)
    lists = make_lists(sources, targets, relation_ids, edge_counts, rows, holders)

    pair = jnp.stack([lists, move(lists, SWAP_Y)])
    lists = jnp.concatenate([pair] + [move(pair, pairs) for pairs in ALONG_Z])
    lists_other = move(lists[:, 1], SWAP_X)

    near = jnp.stack([wire] + [move(wire, pairs) for pairs in FIRST])
    far = move(near, SWAP_CORE)
    local, cross = tiles(plan[0], lists[:, 0], lists[:, 0], relate, near, far)
    total = local + move(cross, SWAP_CORE).astype(F32)
    parts = [move(total[1 + k].astype(BF16), back(FIRST[k])) for k in range(3)]
    master, state, wire = update(master, state, total[0], *parts, width, False)

    near = jnp.stack([wire] + [move(wire, pairs) for pairs in SECOND])
    local, _ = tiles(plan[1], lists[:, 1], lists_other, relate, near, near)
    parts = [move(local[1 + k].astype(BF16), back(SECOND[k])) for k in range(3)]
    entity, state = update(master, state, local[0], *parts, width, True)
    return (entity[None], state)


def shifted(value, axis, steps):
    count = lax.axis_size(axis)
    pairs = [(source, (source + steps) % count) for source in range(count)]
    return lax.ppermute(value, axis, pairs)


def edge_grads(src_rows, dst_rows, rel_rows, live_mask):
    half_width = src_rows.shape[-1] // 2
    source = src_rows.astype(jnp.float32)
    relate = rel_rows.astype(jnp.float32)
    src_real = source[..., :half_width]
    src_imag = source[..., half_width:]
    rel_real = relate[..., :half_width]
    rel_imag = relate[..., half_width:]
    queries = jnp.concatenate(
        [src_real * rel_real - src_imag * rel_imag, src_real * rel_imag + src_imag * rel_real], -1
    ).astype(jnp.bfloat16)
    scores = jnp.einsum("bik,bjk->bij", queries, dst_rows, preferred_element_type=jnp.float32)
    block_size = scores.shape[-1]
    diagonal = jnp.arange(block_size)[:, None] == jnp.arange(block_size)[None, :]
    pair_mask = live_mask[:, :, None] * live_mask[:, None, :]
    weights = (
        jnp.where(diagonal, -jax.nn.sigmoid(-scores), jax.nn.sigmoid(scores) / block_size)
        * pair_mask
    ).astype(jnp.bfloat16)
    query_grad = jnp.einsum("bij,bjk->bik", weights, dst_rows, preferred_element_type=jnp.float32)
    dst_grad = jnp.einsum("bij,bik->bjk", weights, queries, preferred_element_type=jnp.float32)
    grad_real = query_grad[..., :half_width]
    grad_imag = query_grad[..., half_width:]
    src_grad = jnp.concatenate(
        [grad_real * rel_real + grad_imag * rel_imag, grad_imag * rel_real - grad_real * rel_imag],
        -1,
    )
    return (src_grad.astype(jnp.bfloat16), dst_grad.astype(jnp.bfloat16))


def slot_places(row_ids, rows_per, holders_total, capacity):
    holder = row_ids // rows_per
    onehot = (holder[:, None] == jnp.arange(holders_total)[None, :]).astype(jnp.int32)
    running = jnp.cumsum(onehot, axis=0)
    rank = jnp.sum(onehot * running, axis=-1) - 1
    place = holder * capacity + rank
    request = (
        jnp.zeros((holders_total * capacity,), jnp.int32).at[place].set(row_ids - holder * rows_per)
    )
    return (place, request.reshape(holders_total, capacity))


def plain_body(entity_table, adagrad_state, relations, sources, targets, relation_ids, edge_counts):
    entity = entity_table[0]
    adagrad = adagrad_state[0]
    rows_per = entity.shape[0]
    width = entity.shape[1]
    slot_total = sources.shape[-1]
    holders_total = lax.axis_size("row")
    capacity = 2 * slot_total // holders_total
    slot_ids = jnp.arange(slot_total)
    rel_columns = jnp.arange(relations.shape[0])
    for round_index in range(ROUNDS):
        shift_by = round_index + 1
        src_ids = sources[round_index, 0]
        dst_ids = targets[round_index, 0]
        live_total = edge_counts[round_index, 0, 0]
        live_mask = (slot_ids < live_total).astype(jnp.float32)
        rel_onehot = (relation_ids[round_index, 0][:, None] == rel_columns[None, :]).astype(
            jnp.bfloat16
        )
        rel_rows = jnp.dot(rel_onehot, relations, preferred_element_type=jnp.float32).astype(
            jnp.bfloat16
        )
        own_rows = entity.astype(jnp.bfloat16)
        src_place, src_request = slot_places(src_ids, rows_per, holders_total, capacity)
        dst_place, dst_request = slot_places(dst_ids, rows_per, holders_total, capacity)
        serve_table = shifted(own_rows, "dom", shift_by)
        wanted = (
            lax.all_to_all(src_request, "row", split_axis=0, concat_axis=0, tiled=True),
            lax.all_to_all(dst_request, "row", split_axis=0, concat_axis=0, tiled=True),
        )
        src_serve = jnp.take(own_rows, wanted[0].reshape(-1), axis=0).reshape(
            holders_total, capacity, width
        )
        dst_serve = jnp.take(serve_table, wanted[1].reshape(-1), axis=0).reshape(
            holders_total, capacity, width
        )
        answered = (
            lax.all_to_all(src_serve, "row", split_axis=0, concat_axis=0, tiled=True),
            lax.all_to_all(dst_serve, "row", split_axis=0, concat_axis=0, tiled=True),
        )
        dst_answer = answered[1]
        src_rows = jnp.take(answered[0].reshape(-1, width), src_place, axis=0)
        dst_rows = jnp.take(dst_answer.reshape(-1, width), dst_place, axis=0)
        src_grad, dst_grad = edge_grads(
            src_rows.reshape(-1, GROUP, width),
            dst_rows.reshape(-1, GROUP, width),
            rel_rows.reshape(-1, GROUP, width),
            live_mask.reshape(-1, GROUP),
        )
        src_grad = src_grad.reshape(slot_total, width)
        dst_grad = dst_grad.reshape(slot_total, width)
        blank = jnp.zeros((holders_total * capacity, width), jnp.bfloat16)
        src_buffer = blank.at[src_place].set(src_grad).reshape(holders_total, capacity, width)
        dst_buffer = blank.at[dst_place].set(dst_grad).reshape(holders_total, capacity, width)
        parts = (
            lax.all_to_all(src_buffer, "row", split_axis=0, concat_axis=0, tiled=True),
            lax.all_to_all(dst_buffer, "row", split_axis=0, concat_axis=0, tiled=True),
        )
        lhs_sum = jax.ops.segment_sum(
            parts[0].reshape(-1, width).astype(jnp.float32),
            wanted[0].reshape(-1),
            num_segments=rows_per,
        )
        other_sum = jax.ops.segment_sum(
            parts[1].reshape(-1, width).astype(jnp.float32),
            wanted[1].reshape(-1),
            num_segments=rows_per,
        )
        returned = shifted(other_sum, "dom", -shift_by)
        gradient = lhs_sum + returned
        adagrad = adagrad + jnp.mean(gradient * gradient, axis=-1)
        entity = entity - learn_rate * gradient / jnp.sqrt(adagrad)[:, None]
    return (entity[None], adagrad[None])


def solution(mesh):
    in_specs = (
        P("dom", "row", None),
        P("dom", "row"),
        P(),
        P(None, "dom", "row"),
        P(None, "dom", "row"),
        P(None, "dom", "row"),
        P(None, "dom", "row"),
    )
    out_specs = (P("dom", "row", None), P("dom", "row"))

    def body(entity_table, adagrad_state, relations, sources, *rest):
        fits = (
            (mesh.shape["dom"], mesh.shape["row"]) == (4, 8)
            and entity_table.shape[1] == 256
            and sources.shape[-1] == GROUP
        )
        chosen = tile_body if fits else plain_body
        return chosen(entity_table, adagrad_state, relations, sources, *rest)

    return jax.shard_map(body, mesh=mesh, in_specs=in_specs, out_specs=out_specs, check_vma=False)
```

```python
import jax
import jax.numpy as jnp
from jax import lax
from jax.experimental import pallas as pl
from jax.experimental.pallas import tpu as pltpu
from jax.sharding import PartitionSpec as P

GROUP = 384
ROUNDS = 2
LANES = 128
CHUNK = 2 * LANES
NOBODY = 65535

learn_rate = 0.1

F32 = jnp.float32
BF16 = jnp.bfloat16
I32 = jnp.int32
VMEM = pl.BlockSpec(memory_space=pltpu.VMEM)
HBM = pl.BlockSpec(memory_space=pltpu.HBM)
PARAMS = pltpu.CompilerParams(vmem_limit_bytes=48 * 1024 * 1024)


def place(x, core, z, y):
    return (x * 2 + core) * 8 + z * 2 + y


PLACES = [(x, c, z, y) for x in range(2) for c in range(2) for z in range(4) for y in range(2)]


def route(target):
    return [(place(*at), place(*target(*at))) for at in PLACES]


def far_z(x, z, y):
    swap = (z & 1) ^ (z >> 1) ^ y
    return z ^ (3 * swap * (1 - x) + (1 + swap) * x)


FIRST = [
    route(lambda x, c, z, y: (x, c, z ^ 1, y) if c == 0 else (x, c, z, y ^ 1)),
    route(lambda x, c, z, y: (x, c, z ^ 2, y) if c == 0 else (x ^ 1, c, z, y)),
    route(lambda x, c, z, y: (x, c, z ^ 3, y) if c == 0 else (x ^ 1, c, z, y ^ 1)),
]
SWAP_CORE = route(lambda x, c, z, y: (x, c ^ 1, z, y))
SWAP_X = route(lambda x, c, z, y: (x ^ 1, c, z, y))
SWAP_Y = route(lambda x, c, z, y: (x, c, z, y ^ 1))
ALONG_Z = [route(lambda x, c, z, y, k=k: (x, c, z ^ k, y)) for k in (1, 2, 3)]
SECOND = [
    SWAP_Y,
    [(place(x ^ 1, c, far_z(x, z, y), y), place(x, c, z, y)) for x, c, z, y in PLACES],
    [(place(x ^ 1, c, far_z(x, z, y), y ^ 1), place(x, c, z, y)) for x, c, z, y in PLACES],
]


def move(value, pairs):
    return lax.ppermute(value, ("dom", "row"), pairs)


def back(pairs):
    return [(target, source) for source, target in pairs]


def here():
    dom = lax.axis_index("dom")
    row = lax.axis_index("row")
    return dom // 2, dom % 2, row // 2, row % 2


def halves(width):
    half = width // 2
    return half, -(-half // 16) * 16


def spread(value, padded):
    half = value.shape[0] // 2
    blank = jnp.zeros((padded - half, value.shape[1]), value.dtype)
    return jnp.concatenate([value[:half], blank, value[half:], blank], 0)


def open_kernel(
    entity_ref, count_ref, source_ref, target_ref, relation_ref, wire_ref, ids_ref, *scratch
):
    entity, counts, slots, sem = scratch
    refs = (source_ref, target_ref, relation_ref)
    copies = [pltpu.make_async_copy(refs[n], slots.at[n], sem.at[n]) for n in range(3)]
    copies.append(pltpu.make_async_copy(count_ref, counts, sem.at[3]))
    copies.append(pltpu.make_async_copy(entity_ref, entity, sem.at[4]))
    for copy in copies:
        copy.start()
    for copy in copies:
        copy.wait()
    wire_ref[...] = spread(entity[...], wire_ref.shape[0] // 2).astype(BF16)
    edge = lax.broadcasted_iota(I32, (1, ids_ref.shape[1]), 1)
    rows = []
    for round_index in range(ROUNDS):
        live = edge < counts[0:1, round_index : round_index + 1]
        rows.append(jnp.where(live, slots[0, round_index], -1))
        rows.append(jnp.where(live, slots[1, round_index], -1))
        rows.append(slots[2, round_index])
    ids_ref[...] = jnp.concatenate(rows + [jnp.zeros_like(edge)] * 2, 0)


def open_tables(entity, edge_counts, sources, targets, relation_ids):
    width, rows = entity.shape
    padded = halves(width)[1]
    slots = sources.shape[-1]
    return pl.pallas_call(
        open_kernel,
        out_shape=(
            jax.ShapeDtypeStruct((2 * padded, rows), BF16),
            jax.ShapeDtypeStruct((8, slots), I32),
        ),
        in_specs=[HBM] * 5,
        out_specs=(VMEM, VMEM),
        scratch_shapes=[
            pltpu.VMEM((width, rows), F32),
            pltpu.VMEM((1, ROUNDS), I32),
            pltpu.VMEM((3, ROUNDS, 1, slots), I32),
            pltpu.SemaphoreType.DMA((5,)),
        ],
        name="open_tables",
    )(entity, edge_counts.reshape(1, ROUNDS), sources, targets, relation_ids)


def lists_kernel(rows_per, own_ref, other_ref, relations_ref, out_ref, relate_ref):
    slots = own_ref.shape[-1]
    core = lax.axis_index("dom") % 2
    width = relations_ref.shape[1]
    half, padded = halves(width)
    full = -(-width // LANES) * LANES
    relations = jnp.pad(relations_ref[...].astype(F32), ((0, 0), (0, full - width)))
    relate_ref[...] = spread(relations.T[:width], padded).astype(BF16)
    lower = lax.broadcasted_iota(I32, (slots, slots), 0)
    upper = lax.broadcasted_iota(I32, (slots, slots), 1)
    before = (lower <= upper).astype(F32).astype(BF16)
    group_ids = lax.broadcasted_iota(I32, (4, slots), 0)
    edge = lax.broadcasted_iota(I32, (1, 2 * slots), 1)
    found = []
    for round_index in range(ROUNDS):
        for side in range(2):
            along_z = (core == side) if round_index == 0 else False
            parts = []
            for ref in (own_ref, other_ref):
                ids = ref[3 * round_index + side : 3 * round_index + side + 1, :]
                live = ids >= 0
                holder = jnp.where(live, ids // rows_per, 0)
                local = ids - holder * rows_per
                group = holder // 2
                which = holder % 2
                if round_index == 0:
                    group = jnp.where(along_z, holder // 4 * 2 + which, group)
                    which = jnp.where(along_z, holder // 2 % 2, which)
                mine = jnp.logical_and(group_ids == group, live)
                parts.append((live, local, group, which, mine))
            found.append(parts)
    masks = jnp.concatenate(
        [part[4].astype(F32) for parts in found for part in parts], 0
    ).astype(BF16)
    running = jnp.dot(masks, before, preferred_element_type=F32)
    main_ids = lax.broadcasted_iota(I32, (4 * CHUNK, 2 * slots), 0)
    rest_ids = lax.broadcasted_iota(I32, (4 * LANES, 2 * slots), 0) + 4 * CHUNK
    for n, parts in enumerate(found):
        round_index, side = n // 2, n % 2
        joined = []
        first_total = running[8 * n : 8 * n + 4, slots - 1 : slots]
        for which_block, (live, local, group, which, mine) in enumerate(parts):
            ranks = running[8 * n + 4 * which_block : 8 * n + 4 * which_block + 4]
            if which_block == 1:
                ranks = ranks + first_total
            rank = jnp.sum(jnp.where(mine, ranks, 0.0), axis=0, keepdims=True).astype(I32) - 1
            slot = jnp.where(
                rank < CHUNK, group * CHUNK + rank, 4 * CHUNK + group * LANES + rank - CHUNK
            )
            slot = jnp.where(live, slot, -1)
            joined.append((slot, local, which))
        slot, local, which = (
            jnp.concatenate([a, b], 1) for a, b in zip(joined[0], joined[1])
        )
        kind = jnp.concatenate(
            [ref[3 * round_index + 2 : 3 * round_index + 3, :] for ref in (own_ref, other_ref)], 1
        )
        values = jnp.concatenate(
            [local, which, kind, edge // 32, edge % 32, jnp.ones_like(edge)]
            + [jnp.zeros_like(edge)] * 2,
            0,
        ).astype(F32).astype(BF16)

        def place_rows(slot_ids, first_row):
            pick = (slot_ids == slot).astype(F32).astype(BF16)
            rows = lax.dot_general(
                values, pick, (((1,), (1,)), ((), ())), preferred_element_type=F32
            ).astype(I32)
            there = rows[5:6] > 0
            ids = jnp.where(there, rows[1:2] * rows_per + rows[0:1], NOBODY)
            packed = jnp.bitwise_or(ids, jnp.left_shift(rows[3:4] * 32 + rows[4:5], 16))
            for at in range(slot_ids.shape[0] // LANES):
                cut = slice(at * LANES, (at + 1) * LANES)
                row = first_row + at
                out_ref[round_index, 2 * side, row : row + 1, :] = packed[:, cut]
                if side == 0:
                    out_ref[round_index, 1, row : row + 1, :] = rows[2:3, cut]

        place_rows(main_ids, 0)
        out_ref[round_index, 2 * side, 8:12, :] = jnp.full((4, LANES), NOBODY, I32)
        if side == 0:
            out_ref[round_index, 1, 8:12, :] = jnp.zeros((4, LANES), I32)

        @pl.when(jnp.max(slot) >= 4 * CHUNK)
        def _():
            place_rows(rest_ids, 8)


def make_lists(own, other, relations, rows_per):
    width = relations.shape[1]

    def kernel(*refs):
        lists_kernel(rows_per, *refs)

    return pl.pallas_call(
        kernel,
        out_shape=(
            jax.ShapeDtypeStruct((ROUNDS, 3, 12, LANES), I32),
            jax.ShapeDtypeStruct((2 * halves(width)[1], relations.shape[0]), BF16),
        ),
        in_specs=[VMEM] * 3,
        out_specs=(VMEM, VMEM),
        compiler_params=PARAMS,
        name="make_lists",
    )(own, other, relations)


def both(left, right):
    return jnp.concatenate([left, right], 0)


def tile(source, target, relate, source_edge, target_edge):
    half = source.shape[0] // 2
    relate_re, relate_im = relate[:half], relate[half:]
    source_re, source_im = source[:half].astype(F32), source[half:].astype(F32)
    queries = both(
        source_re * relate_re - source_im * relate_im,
        source_re * relate_im + source_im * relate_re,
    ).astype(BF16)
    scores = lax.dot_general(
        queries, target, (((0,), (0,)), ((), ())), preferred_element_type=F32
    )
    edge_row = target_edge.astype(F32)
    edge_col = jnp.broadcast_to(source_edge.astype(F32), (8, source_edge.shape[1])).T[:, :1]
    bent = 0.5 * jnp.tanh(0.5 * scores)
    weights = jnp.where(
        edge_col == edge_row,
        bent - 0.5,
        jnp.where((edge_col < GROUP) == (edge_row < GROUP), (bent + 0.5) * (1.0 / GROUP), 0.0),
    ).astype(BF16)
    query_grad = lax.dot_general(
        target, weights, (((1,), (1,)), ((), ())), preferred_element_type=F32
    )
    target_grad = jnp.dot(queries, weights, preferred_element_type=F32).astype(BF16)
    grad_re, grad_im = query_grad[:half], query_grad[half:]
    source_grad = both(
        grad_re * relate_re + grad_im * relate_im,
        grad_im * relate_re - grad_re * relate_im,
    ).astype(BF16)
    return source_grad, target_grad


def wanted_lists(round_index):
    x, core, z, y = here()
    if round_index == 0:
        line = z // 2 * 2 + y
        other_line = (1 - z // 2) * 2 + y
        return [(0, core, line), (0, core, other_line), (0, 1 - core, z)]
    swap = (z % 2 + z // 2 + y) % 2
    far = jnp.bitwise_xor(z, jnp.where(x == 0, 3 * swap, 1 + swap))
    return [(0, 0, z), (0, 1, far), (1, 0, far), (1, 1, z)]


def tiles_kernel(round_index, *refs):
    count = 4 if round_index == 0 else 2
    list_refs, relations_ref, refs = refs[:count], refs[count], refs[count + 1 :]
    count = 8 if round_index == 0 else 4
    table_refs, out_refs = refs[:count], refs[count : 2 * count]
    lists, flags, tables, picks, values, sums = refs[2 * count :]
    padded, rows = table_refs[0].shape
    pairs = lists.shape[1]
    x, core, z, y = here()
    low = z % 2
    wanted = wanted_lists(round_index)
    total = len(wanted)
    for pair in range(pairs):
        if round_index == 0:
            lists[0, pair] = list_refs[pair][0]
        else:
            lists[0, pair] = list_refs[0][pair]
            lists[1, pair] = list_refs[1][pair]

    def choose(flag, first, second):
        return jnp.where(flag == 0, first, second)

    def lay(n, flag, first, second):
        tables[n, :, :rows] = choose(flag, first[...], second[...])
        tables[n, :, rows:] = choose(flag, second[...], first[...])

    if round_index == 0:
        near, far = table_refs[:4], table_refs[4:]

        @pl.when(core == 0)
        def _():
            lay(0, low, near[0], near[1])
            lay(1, low, near[2], near[3])
            lay(2, y, far[2], far[3])

        @pl.when(core == 1)
        def _():
            lay(0, low, far[0], far[1])
            lay(1, low, far[2], far[3])
            lay(2, y, near[0], near[1])
    else:
        for n, first in ((0, 0), (1, 2), (2, 2), (3, 0)):
            lay(n, y, table_refs[first], table_refs[first + 1])

    def packed_of(n, pair):
        bucket, side, group = wanted[n]
        return jnp.concatenate(
            [lists[bucket, pair, 2 * side, pl.ds(2 * group + j, 1), :] for j in range(2)], 1
        )

    def kinds_of(n, pair):
        bucket, _, group = wanted[n]
        return jnp.concatenate(
            [lists[bucket, pair, 1, pl.ds(2 * group + j, 1), :] for j in range(2)], 1
        )

    row_ids = lax.broadcasted_iota(I32, (2 * rows, CHUNK), 0)

    def pick_of(packed):
        return (row_ids == jnp.bitwise_and(packed, 65535)).astype(F32).astype(BF16)

    def relate_of(kinds):
        slots = lax.broadcasted_iota(I32, (relations_ref.shape[1], kinds.shape[1]), 0)
        chosen = (slots == kinds).astype(F32).astype(BF16)
        return jnp.dot(relations_ref[...], chosen, preferred_element_type=F32)

    for n in range(total):
        for pair in range(pairs):
            cut = slice(pair * CHUNK, (pair + 1) * CHUNK)
            picks[n, :, cut] = pick_of(packed_of(n, pair))
        values[n] = jnp.dot(tables[n], picks[n], preferred_element_type=F32).astype(BF16)

    def compute(pair, sources, targets):
        cut = slice(pair * CHUNK, (pair + 1) * CHUNK)

        def joined(chosen, get):
            return jnp.concatenate([get(n) for n in chosen], 1)

        def edges(chosen):
            return joined(chosen, lambda n: jnp.right_shift(packed_of(n, pair), 16))

        got = tile(
            joined(sources, lambda n: values[n, :, cut]),
            joined(targets, lambda n: values[n, :, cut]),
            relate_of(joined(sources, lambda n: kinds_of(n, pair))),
            edges(sources),
            edges(targets),
        )
        for chosen, grads in zip((sources, targets), got):
            for at, n in enumerate(chosen):
                values[n, :, cut] = grads[:, at * CHUNK : (at + 1) * CHUNK]

    if round_index == 0:

        @pl.when(core == 0)
        def _():
            for pair in range(pairs):
                compute(pair, (0, 1), (2,))

        @pl.when(core == 1)
        def _():
            for pair in range(pairs):
                compute(pair, (2,), (0, 1))
    else:
        for pair in range(pairs):
            compute(pair, (0,), (1,))
            compute(pair, (2,), (3,))

    def scatter(grads, pick):
        return lax.dot_general(grads, pick, (((1,), (1,)), ((), ())), preferred_element_type=F32)

    for n in range(total):
        sums[n] = scatter(values[n], picks[n])

    def late_row(n, pair, kind):
        bucket, _, group = wanted[n]
        return lists[bucket, pair, kind, pl.ds(8 + group, 1), :]

    def late_ids(n, pair):
        return jnp.bitwise_and(late_row(n, pair, 2 * wanted[n][1]), 65535)

    lowest = late_ids(0, 0)
    for n in range(total):
        for pair in range(pairs):
            lowest = jnp.minimum(lowest, late_ids(n, pair))

    @pl.when(jnp.min(lowest) < NOBODY)
    def _():
        for n in range(total):
            for pair in range(pairs):
                flags[n, pair] = (jnp.min(late_ids(n, pair)) < NOBODY).astype(I32)
        spare = jnp.full((1, LANES), NOBODY, I32)

        def one_of(options, at):
            value = options[0]
            for n in range(1, len(options)):
                value = jnp.where(at == n, options[n], value)
            return value

        def each(step, carry):
            pair, task, combo = step // 6, step // 3 % 2, step % 3
            if round_index == 0:
                chosen = (jnp.where(core == 0, task, 2), jnp.where(core == 0, 2, task))
            else:
                chosen = (2 * task, 2 * task + 1)
            late = (combo != 1, combo != 0)
            due = [
                jnp.logical_or(jnp.logical_not(late[side]), flags[chosen[side], pair] > 0)
                for side in range(2)
            ]

            @pl.when(jnp.logical_and(due[0], due[1]))
            def _():
                found = []
                for side in range(2):
                    main = one_of([packed_of(n, pair) for n in range(total)], chosen[side])
                    extra = one_of(
                        [late_row(n, pair, 2 * wanted[n][1]) for n in range(total)], chosen[side]
                    )
                    packed = jnp.where(late[side], jnp.concatenate([extra, spare], 1), main)
                    pick = pick_of(packed)
                    gathered = jnp.dot(tables[chosen[side]], pick, preferred_element_type=F32)
                    found.append((gathered.astype(BF16), pick, jnp.right_shift(packed, 16)))
                main = one_of([kinds_of(n, pair) for n in range(total)], chosen[0])
                extra = one_of([late_row(n, pair, 1) for n in range(total)], chosen[0])
                kinds = jnp.where(late[0], jnp.concatenate([extra, extra], 1), main)
                grads = tile(
                    found[0][0], found[1][0], relate_of(kinds), found[0][2], found[1][2]
                )
                for side in range(2):
                    sums[chosen[side]] += scatter(grads[side], found[side][1])

            return carry

        lax.fori_loop(0, pairs * 6, each, 0)

    def part(total, which):
        return choose(which, total[:, :rows], total[:, rows:])

    if round_index > 0:
        near = sums[0] + sums[3]
        far = sums[1] + sums[2]
        out_refs[0][...] = part(near, y)
        out_refs[1][...] = part(near, 1 - y).astype(BF16)
        out_refs[2][...] = part(far, y).astype(BF16)
        out_refs[3][...] = part(far, 1 - y).astype(BF16)
        return

    def put(outs, n, which):
        for k in range(2):
            outs[k][...] = part(sums[n], which if k == 0 else 1 - which).astype(outs[k].dtype)

    def clear(outs):
        for ref in outs:
            ref[...] = jnp.zeros(ref.shape, ref.dtype)

    @pl.when(core == 0)
    def _():
        put(out_refs[0:2], 0, low)
        put(out_refs[2:4], 1, low)
        clear(out_refs[4:6])
        put(out_refs[6:8], 2, y)

    @pl.when(core == 1)
    def _():
        put(out_refs[0:2], 2, y)
        clear(out_refs[2:4])
        put(out_refs[4:6], 0, low)
        put(out_refs[6:8], 1, low)


def tiles(round_index, lists, relations, tables):
    padded, rows = tables[0].shape
    total, pairs = 3 + round_index, 4

    def kernel(*refs):
        tiles_kernel(round_index, *refs)

    kinds = [F32] * 4 + [BF16] * 4 if round_index == 0 else [F32] + [BF16] * 3
    operands = (*lists, relations, *tables)
    return pl.pallas_call(
        kernel,
        out_shape=tuple(jax.ShapeDtypeStruct((padded, rows), kind) for kind in kinds),
        in_specs=[VMEM] * len(operands),
        out_specs=(VMEM,) * len(kinds),
        scratch_shapes=[
            pltpu.VMEM((2, pairs, 3, 12, LANES), I32),
            pltpu.SMEM((4, pairs), I32),
            pltpu.VMEM((total, padded, 2 * rows), BF16),
            pltpu.VMEM((total, 2 * rows, pairs * CHUNK), BF16),
            pltpu.VMEM((total, padded, pairs * CHUNK), BF16),
            pltpu.VMEM((total, padded, 2 * rows), F32),
        ],
        compiler_params=PARAMS,
        cost_estimate=pl.CostEstimate(
            flops=8_000_000_000, bytes_accessed=8_000_000, transcendentals=1_000_000
        ),
        name="tiles",
    )(*operands)


def update_kernel(master_ref, state_ref, own_ref, a_ref, b_ref, c_ref, *outs):
    width = master_ref.shape[0]
    half, padded = halves(width)
    gradient = (own_ref[...] + a_ref[...].astype(F32)) + (
        b_ref[...].astype(F32) + c_ref[...].astype(F32)
    )
    gradient = jnp.concatenate([gradient[:half], gradient[padded : padded + half]], 0)
    state = state_ref[...] + jnp.sum(gradient * gradient, axis=0, keepdims=True) / width
    master = master_ref[...] - gradient * (learn_rate / jnp.sqrt(state))
    outs[0][...] = master
    outs[1][...] = state
    if len(outs) > 2:
        outs[2][...] = spread(master, padded).astype(BF16)


def update(master, state, own, a, b, c, last):
    shapes = [(master.shape, F32), (state.shape, F32)]
    if not last:
        shapes.append((own.shape, BF16))
    return pl.pallas_call(
        update_kernel,
        out_shape=tuple(jax.ShapeDtypeStruct(*shape) for shape in shapes),
        in_specs=[VMEM] * 6,
        out_specs=(VMEM,) * len(shapes),
        compiler_params=PARAMS,
        name="update",
    )(master, state, own, a, b, c)


def tied(value, other):
    return lax.optimization_barrier((value, other))[0]


def tile_body(entity_table, adagrad_state, relations, sources, targets, relation_ids, edge_counts):
    rows = entity_table.shape[1]
    entity = entity_table[0].T
    state = adagrad_state
    wire, ids = open_tables(entity, edge_counts, sources, targets, relation_ids)

    other_ids = move(ids, SWAP_Y)
    near = [wire] + [move(wire, pairs) for pairs in FIRST]
    lists, relate = make_lists(ids, other_ids, relations, rows)
    lists = [lists] + [move(lists, pairs) for pairs in ALONG_Z]
    *near, _ = lax.optimization_barrier((*near, lists))
    far = [move(block, SWAP_CORE) for block in near]
    second_lists = jnp.stack([part[1] for part in lists])
    other_lists = move(second_lists, SWAP_X)

    first = lax.optimization_barrier((lists, second_lists))[0]
    outs = tiles(0, first, relate, near + far)
    outs, other_lists = lax.optimization_barrier((outs, other_lists))
    cross = [move(block, SWAP_CORE).astype(F32) for block in outs[4:]]
    parts = [
        move((outs[1 + k] + cross[1 + k]).astype(BF16), back(FIRST[k])) for k in range(3)
    ]
    entity, state, wire = update(entity, state, outs[0] + cross[0], *parts, False)

    near = [wire] + [move(wire, pairs) for pairs in SECOND]
    own, *parts = tiles(1, [second_lists, other_lists], relate, near)
    parts = [move(parts[k], back(SECOND[k])) for k in range(3)]
    entity, state = update(entity, state, own, *parts, True)
    return (entity.T[None], state)


def shifted(value, axis, steps):
    count = lax.axis_size(axis)
    pairs = [(source, (source + steps) % count) for source in range(count)]
    return lax.ppermute(value, axis, pairs)


def edge_grads(src_rows, dst_rows, rel_rows, live_mask):
    half_width = src_rows.shape[-1] // 2
    source = src_rows.astype(jnp.float32)
    relate = rel_rows.astype(jnp.float32)
    src_real = source[..., :half_width]
    src_imag = source[..., half_width:]
    rel_real = relate[..., :half_width]
    rel_imag = relate[..., half_width:]
    queries = jnp.concatenate(
        [src_real * rel_real - src_imag * rel_imag, src_real * rel_imag + src_imag * rel_real], -1
    ).astype(jnp.bfloat16)
    scores = jnp.einsum("bik,bjk->bij", queries, dst_rows, preferred_element_type=jnp.float32)
    block_size = scores.shape[-1]
    diagonal = jnp.arange(block_size)[:, None] == jnp.arange(block_size)[None, :]
    pair_mask = live_mask[:, :, None] * live_mask[:, None, :]
    weights = (
        jnp.where(diagonal, -jax.nn.sigmoid(-scores), jax.nn.sigmoid(scores) / block_size)
        * pair_mask
    ).astype(jnp.bfloat16)
    query_grad = jnp.einsum("bij,bjk->bik", weights, dst_rows, preferred_element_type=jnp.float32)
    dst_grad = jnp.einsum("bij,bik->bjk", weights, queries, preferred_element_type=jnp.float32)
    grad_real = query_grad[..., :half_width]
    grad_imag = query_grad[..., half_width:]
    src_grad = jnp.concatenate(
        [grad_real * rel_real + grad_imag * rel_imag, grad_imag * rel_real - grad_real * rel_imag],
        -1,
    )
    return (src_grad.astype(jnp.bfloat16), dst_grad.astype(jnp.bfloat16))


def slot_places(row_ids, rows_per, holders_total, capacity):
    holder = row_ids // rows_per
    onehot = (holder[:, None] == jnp.arange(holders_total)[None, :]).astype(jnp.int32)
    running = jnp.cumsum(onehot, axis=0)
    rank = jnp.sum(onehot * running, axis=-1) - 1
    place = holder * capacity + rank
    request = (
        jnp.zeros((holders_total * capacity,), jnp.int32).at[place].set(row_ids - holder * rows_per)
    )
    return (place, request.reshape(holders_total, capacity))


def plain_body(entity_table, adagrad_state, relations, sources, targets, relation_ids, edge_counts):
    entity = entity_table[0]
    adagrad = adagrad_state[0]
    rows_per = entity.shape[0]
    width = entity.shape[1]
    slot_total = sources.shape[-1]
    holders_total = lax.axis_size("row")
    capacity = 2 * slot_total // holders_total
    slot_ids = jnp.arange(slot_total)
    rel_columns = jnp.arange(relations.shape[0])
    for round_index in range(ROUNDS):
        shift_by = round_index + 1
        src_ids = sources[round_index, 0]
        dst_ids = targets[round_index, 0]
        live_total = edge_counts[round_index, 0, 0]
        live_mask = (slot_ids < live_total).astype(jnp.float32)
        rel_onehot = (relation_ids[round_index, 0][:, None] == rel_columns[None, :]).astype(
            jnp.bfloat16
        )
        rel_rows = jnp.dot(rel_onehot, relations, preferred_element_type=jnp.float32).astype(
            jnp.bfloat16
        )
        own_rows = entity.astype(jnp.bfloat16)
        src_place, src_request = slot_places(src_ids, rows_per, holders_total, capacity)
        dst_place, dst_request = slot_places(dst_ids, rows_per, holders_total, capacity)
        serve_table = shifted(own_rows, "dom", shift_by)
        wanted = (
            lax.all_to_all(src_request, "row", split_axis=0, concat_axis=0, tiled=True),
            lax.all_to_all(dst_request, "row", split_axis=0, concat_axis=0, tiled=True),
        )
        src_serve = jnp.take(own_rows, wanted[0].reshape(-1), axis=0).reshape(
            holders_total, capacity, width
        )
        dst_serve = jnp.take(serve_table, wanted[1].reshape(-1), axis=0).reshape(
            holders_total, capacity, width
        )
        answered = (
            lax.all_to_all(src_serve, "row", split_axis=0, concat_axis=0, tiled=True),
            lax.all_to_all(dst_serve, "row", split_axis=0, concat_axis=0, tiled=True),
        )
        dst_answer = answered[1]
        src_rows = jnp.take(answered[0].reshape(-1, width), src_place, axis=0)
        dst_rows = jnp.take(dst_answer.reshape(-1, width), dst_place, axis=0)
        src_grad, dst_grad = edge_grads(
            src_rows.reshape(-1, GROUP, width),
            dst_rows.reshape(-1, GROUP, width),
            rel_rows.reshape(-1, GROUP, width),
            live_mask.reshape(-1, GROUP),
        )
        src_grad = src_grad.reshape(slot_total, width)
        dst_grad = dst_grad.reshape(slot_total, width)
        blank = jnp.zeros((holders_total * capacity, width), jnp.bfloat16)
        src_buffer = blank.at[src_place].set(src_grad).reshape(holders_total, capacity, width)
        dst_buffer = blank.at[dst_place].set(dst_grad).reshape(holders_total, capacity, width)
        parts = (
            lax.all_to_all(src_buffer, "row", split_axis=0, concat_axis=0, tiled=True),
            lax.all_to_all(dst_buffer, "row", split_axis=0, concat_axis=0, tiled=True),
        )
        lhs_sum = jax.ops.segment_sum(
            parts[0].reshape(-1, width).astype(jnp.float32),
            wanted[0].reshape(-1),
            num_segments=rows_per,
        )
        other_sum = jax.ops.segment_sum(
            parts[1].reshape(-1, width).astype(jnp.float32),
            wanted[1].reshape(-1),
            num_segments=rows_per,
        )
        returned = shifted(other_sum, "dom", -shift_by)
        gradient = lhs_sum + returned
        adagrad = adagrad + jnp.mean(gradient * gradient, axis=-1)
        entity = entity - learn_rate * gradient / jnp.sqrt(adagrad)[:, None]
    return (entity[None], adagrad[None])


def solution(mesh):
    in_specs = (
        P("dom", "row", None),
        P("dom", "row"),
        P(),
        P(None, "dom", "row"),
        P(None, "dom", "row"),
        P(None, "dom", "row"),
        P(None, "dom", "row"),
    )
    out_specs = (P("dom", "row", None), P("dom", "row"))

    def body(entity_table, adagrad_state, relations, sources, *rest):
        fits = (
            (mesh.shape["dom"], mesh.shape["row"]) == (4, 8)
            and entity_table.shape[1] == 256
            and sources.shape[-1] == GROUP
        )
        chosen = tile_body if fits else plain_body
        return chosen(entity_table, adagrad_state, relations, sources, *rest)

    return jax.shard_map(body, mesh=mesh, in_specs=in_specs, out_specs=out_specs, check_vma=False)
```

```python
import jax
import jax.numpy as jnp
from jax import lax
from jax.experimental import pallas as pl
from jax.experimental.pallas import tpu as pltpu
from jax.sharding import PartitionSpec as P

GROUP = 384
ROUNDS = 2
LANES = 128
CHUNK = 2 * LANES
NOBODY = 65535
DEAD = 32767

learn_rate = 0.1

F32 = jnp.float32
BF16 = jnp.bfloat16
I32 = jnp.int32
VMEM = pl.BlockSpec(memory_space=pltpu.VMEM)
HBM = pl.BlockSpec(memory_space=pltpu.HBM)
PARAMS = pltpu.CompilerParams(vmem_limit_bytes=48 * 1024 * 1024)


def place(x, core, z, y):
    return (x * 2 + core) * 8 + z * 2 + y


PLACES = [(x, c, z, y) for x in range(2) for c in range(2) for z in range(4) for y in range(2)]


def route(target):
    return [(place(*at), place(*target(*at))) for at in PLACES]


def far_z(x, z, y):
    swap = (z & 1) ^ (z >> 1) ^ y
    return z ^ (3 * swap * (1 - x) + (1 + swap) * x)


FIRST = [
    route(lambda x, c, z, y: (x, c, z ^ 1, y) if c == 0 else (x, c, z, y ^ 1)),
    route(lambda x, c, z, y: (x, c, z ^ 2, y) if c == 0 else (x ^ 1, c, z, y)),
    route(lambda x, c, z, y: (x, c, z ^ 3, y) if c == 0 else (x ^ 1, c, z, y ^ 1)),
]
SWAP_CORE = route(lambda x, c, z, y: (x, c ^ 1, z, y))
SWAP_X = route(lambda x, c, z, y: (x ^ 1, c, z, y))
SWAP_Y = route(lambda x, c, z, y: (x, c, z, y ^ 1))
SECOND = [
    SWAP_Y,
    [(place(x ^ 1, c, far_z(x, z, y), y), place(x, c, z, y)) for x, c, z, y in PLACES],
    [(place(x ^ 1, c, far_z(x, z, y), y ^ 1), place(x, c, z, y)) for x, c, z, y in PLACES],
]


def move(value, pairs):
    return lax.ppermute(value, ("dom", "row"), pairs)


def back(pairs):
    return [(target, source) for source, target in pairs]


def here():
    dom = lax.axis_index("dom")
    row = lax.axis_index("row")
    return dom // 2, dom % 2, row // 2, row % 2


def halves(width):
    half = width // 2
    return half, -(-half // 16) * 16


def spread(value, padded):
    half = value.shape[0] // 2
    blank = jnp.zeros((padded - half, value.shape[1]), value.dtype)
    return jnp.concatenate([value[:half], blank, value[half:], blank], 0)


def open_kernel(
    entity_ref, count_ref, source_ref, target_ref, relation_ref, wire_ref, ids_ref, *scratch
):
    entity, counts, slots, sem = scratch
    refs = (source_ref, target_ref, relation_ref)
    copies = [pltpu.make_async_copy(refs[n], slots.at[n], sem.at[n]) for n in range(3)]
    copies.append(pltpu.make_async_copy(count_ref, counts, sem.at[3]))
    copies.append(pltpu.make_async_copy(entity_ref, entity, sem.at[4]))
    for copy in copies:
        copy.start()
    for copy in copies:
        copy.wait()
    wire_ref[...] = spread(entity[...], wire_ref.shape[0] // 2).astype(BF16)
    edge = lax.broadcasted_iota(I32, (1, ids_ref.shape[2]), 1)
    rows, kinds = [], []
    for round_index in range(ROUNDS):
        live = edge < counts[0:1, round_index : round_index + 1]
        source = jnp.where(live, slots[0, round_index], DEAD)
        target = jnp.where(live, slots[1, round_index], DEAD)
        rows.append(jnp.bitwise_or(source, jnp.left_shift(target, 16)))
        kinds.append(slots[2, round_index])
    rows.append(jnp.bitwise_or(kinds[0], jnp.left_shift(kinds[1], 16)))
    ids = jnp.concatenate(rows + [jnp.zeros_like(edge)], 0)
    for n in range(ids_ref.shape[0]):
        ids_ref[n] = ids


def open_tables(entity, edge_counts, sources, targets, relation_ids, copies):
    width, rows = entity.shape
    padded = halves(width)[1]
    slots = sources.shape[-1]
    return pl.pallas_call(
        open_kernel,
        out_shape=(
            jax.ShapeDtypeStruct((2 * padded, rows), BF16),
            jax.ShapeDtypeStruct((copies, 4, slots), I32),
        ),
        in_specs=[HBM] * 5,
        out_specs=(VMEM, VMEM),
        scratch_shapes=[
            pltpu.VMEM((width, rows), F32),
            pltpu.VMEM((1, ROUNDS), I32),
            pltpu.VMEM((3, ROUNDS, 1, slots), I32),
            pltpu.SemaphoreType.DMA((5,)),
        ],
        name="open_tables",
    )(entity, edge_counts.reshape(1, ROUNDS), sources, targets, relation_ids)


def wanted_lists(round_index):
    x, core, z, y = here()
    if round_index == 0:
        line = z // 2 * 2 + y
        other_line = (1 - z // 2) * 2 + y
        return [(0, core, line), (0, core, other_line), (0, 1 - core, z)]
    swap = (z % 2 + z // 2 + y) % 2
    far = jnp.bitwise_xor(z, jnp.where(x == 0, 3 * swap, 1 + swap))
    return [(0, 0, z), (0, 1, far), (1, 0, far), (1, 1, z)]


def lists_kernel(round_index, rows_per, *refs):
    buckets = 1 if round_index == 0 else 2
    id_refs, (relations_ref, out_ref, *relate_ref) = refs[:buckets], refs[buckets:]
    blocks, _, slots = id_refs[0].shape
    pairs = blocks // 2
    lists = wanted_lists(round_index)
    if relate_ref:
        width = relations_ref.shape[1]
        half, padded = halves(width)
        full = -(-width // LANES) * LANES
        relations = jnp.pad(relations_ref[...].astype(F32), ((0, 0), (0, full - width)))
        relate_ref[0][...] = spread(relations.T[:width], padded).astype(BF16)
    lower = lax.broadcasted_iota(I32, (slots, slots), 0)
    upper = lax.broadcasted_iota(I32, (slots, slots), 1)
    before = (lower <= upper).astype(F32).astype(BF16)
    edge = lax.broadcasted_iota(I32, (1, slots), 1)
    one = jnp.ones_like(edge)
    order = [(n, pair) for n in range(len(lists)) for pair in range(pairs)]

    values, masks = [], []
    for ref in id_refs:
        packed = jnp.concatenate([ref[b, round_index : round_index + 1, :] for b in range(blocks)], 0)
        kinds = jnp.concatenate([ref[b, 2:3, :] for b in range(blocks)], 0)
        kinds = jnp.bitwise_and(jnp.right_shift(kinds, 16 * round_index), 65535)
        sides = [jnp.bitwise_and(packed, 65535), jnp.right_shift(packed, 16)]
        values.append((sides, kinds))
    spots = []
    for bucket, side, group in lists:
        sides, kinds = values[bucket]
        if round_index == 0:
            ids = jnp.where(side == 0, sides[0], sides[1])
        else:
            ids = sides[side]
        live = sides[0] != DEAD
        holder = ids // rows_per
        local = jnp.where(live, ids - holder * rows_per, 0)
        if round_index == 0 and len(spots) < 2:
            mine = holder // 4 * 2 + holder % 2 == group
            which = holder // 2 % 2
        else:
            mine = holder // 2 == group
            which = holder % 2
        mine = jnp.logical_and(mine, live)
        spots.append((local, jnp.where(live, which, 0), mine, kinds))
        for k in range(2):
            masks.append(jnp.logical_and(mine, which == k).astype(F32))
    stacked = jnp.concatenate(masks, 0).astype(BF16)
    running = jnp.dot(stacked, before, preferred_element_type=F32)
    slots_of, late = [], []
    for n, (local, which, mine, kinds) in enumerate(spots):
        even, odd = (
            running[(2 * n + k) * blocks : (2 * n + k + 1) * blocks] for k in range(2)
        )
        second = lax.broadcasted_iota(I32, (blocks, 1), 0) % 2 == 1
        totals = [part[:, slots - 1 : slots] for part in (even, odd)]
        ahead = [
            jnp.concatenate([total[:1], total[:-1]], 0) for total in totals
        ]
        behind = [jnp.concatenate([total[1:], total[:1]], 0) for total in totals]
        whole = [
            total + jnp.where(second, a, b) for total, a, b in zip(totals, ahead, behind)
        ]
        even = even + jnp.where(second, ahead[0], 0.0)
        odd = odd + jnp.where(second, ahead[1], 0.0)
        room = CHUNK - whole[1]
        slot = jnp.where(
            which == 1, CHUNK - odd, jnp.where(even <= room, even - 1, CHUNK + even - 1 - room)
        )
        slots_of.append(jnp.where(mine, slot, -1.0))
        bit = lax.broadcasted_iota(I32, (blocks, 1), 0) // 2 + pairs * n
        over = jnp.logical_and(jnp.logical_not(second), whole[0] > room)
        late.append(jnp.where(over, jnp.left_shift(jnp.ones_like(bit), bit), 0))
    late = jnp.sum(jnp.concatenate(late, 0))
    chunk_ids = lax.broadcasted_iota(I32, (CHUNK, 2 * slots), 0).astype(F32)
    late_ids = lax.broadcasted_iota(I32, (LANES, 2 * slots), 0).astype(F32) + CHUNK
    edges = jnp.concatenate([edge, edge + slots], 1)
    nobody = jnp.full((1, LANES), NOBODY, I32)
    blank = jnp.zeros((1, LANES), I32)
    for n, (local, which, mine, kinds) in enumerate(spots):
        for pair in range(pairs):

            def joined(part, pair=pair):
                return jnp.concatenate([part[2 * pair : 2 * pair + 1], part[2 * pair + 1 : 2 * pair + 2]], 1)

            slot = joined(slots_of[n])
            columns = (
                jnp.concatenate(
                    [
                        joined(local),
                        joined(which),
                        joined(kinds),
                        edges // 32,
                        edges % 32,
                        jnp.ones_like(edges),
                    ]
                    + [jnp.zeros_like(edges)] * 2,
                    0,
                )
                .astype(F32)
                .astype(BF16)
            )

            def rows_at(slot_ids, slot=slot, columns=columns):
                chosen = (slot_ids == slot).astype(F32).astype(BF16)
                got = lax.dot_general(
                    columns, chosen, (((1,), (1,)), ((), ())), preferred_element_type=F32
                ).astype(I32)
                ids = jnp.where(got[5:6] > 0, got[1:2] * rows_per + got[0:1], NOBODY)
                return jnp.bitwise_or(ids, jnp.left_shift(got[3:4] * 32 + got[4:5], 16)), got[2:3]

            packed, kind = rows_at(chunk_ids)
            for k in range(2):
                cut = slice(k * LANES, (k + 1) * LANES)
                out_ref[n, pair, k : k + 1, :] = packed[:, cut]
                out_ref[n, pair, 3 + k : 4 + k, :] = kind[:, cut]
            out_ref[n, pair, 2:3, :] = nobody
            out_ref[n, pair, 5:6, :] = blank

            @pl.when(jnp.bitwise_and(jnp.right_shift(late, pairs * n + pair), 1) > 0)
            def _():
                packed, kind = rows_at(late_ids)
                out_ref[n, pair, 2:3, :] = packed
                out_ref[n, pair, 5:6, :] = kind


def make_lists(round_index, ids, relations, rows_per):
    width = relations.shape[1]

    def kernel(*refs):
        lists_kernel(round_index, rows_per, *refs)

    shapes = [jax.ShapeDtypeStruct((3 + round_index, ids[0].shape[0] // 2, 8, LANES), I32)]
    if round_index == 0:
        shapes.append(jax.ShapeDtypeStruct((2 * halves(width)[1], relations.shape[0]), BF16))
    return pl.pallas_call(
        kernel,
        out_shape=tuple(shapes),
        in_specs=[VMEM] * (len(ids) + 1),
        out_specs=(VMEM,) * len(shapes),
        compiler_params=PARAMS,
        cost_estimate=pl.CostEstimate(
            flops=4_000_000_000, bytes_accessed=1_000_000, transcendentals=0
        ),
        name="make_lists",
    )(*ids, relations)


def both(left, right):
    return jnp.concatenate([left, right], 0)


def tile(source, target, relate, source_edge, target_edge):
    half = source.shape[0] // 2
    relate_re, relate_im = relate[:half], relate[half:]
    source_re, source_im = source[:half].astype(F32), source[half:].astype(F32)
    queries = both(
        source_re * relate_re - source_im * relate_im,
        source_re * relate_im + source_im * relate_re,
    ).astype(BF16)
    scores = lax.dot_general(
        queries, target, (((0,), (0,)), ((), ())), preferred_element_type=F32
    )
    edge_row = target_edge.astype(F32)
    edge_col = jnp.broadcast_to(source_edge.astype(F32), (8, source_edge.shape[1])).T[:, :1]
    bent = 0.5 * jnp.tanh(0.5 * scores)
    weights = jnp.where(
        edge_col == edge_row,
        bent - 0.5,
        jnp.where((edge_col < GROUP) == (edge_row < GROUP), (bent + 0.5) * (1.0 / GROUP), 0.0),
    ).astype(BF16)
    query_grad = lax.dot_general(
        target, weights, (((1,), (1,)), ((), ())), preferred_element_type=F32
    )
    target_grad = jnp.dot(queries, weights, preferred_element_type=F32).astype(BF16)
    grad_re, grad_im = query_grad[:half], query_grad[half:]
    source_grad = both(
        grad_re * relate_re + grad_im * relate_im,
        grad_im * relate_re - grad_re * relate_im,
    ).astype(BF16)
    return source_grad, target_grad


def tiles_kernel(round_index, *refs):
    lists, relations_ref, refs = refs[0], refs[1], refs[2:]
    count = 8 if round_index == 0 else 4
    table_refs, out_refs = refs[:count], refs[count : 2 * count]
    tables, picks, values, sums = refs[2 * count :]
    padded, rows = table_refs[0].shape
    total, pairs = lists.shape[:2]
    x, core, z, y = here()
    low = z % 2

    def choose(flag, first, second):
        return jnp.where(flag == 0, first, second)

    def lay(n, flag, first, second):
        tables[n, :, :rows] = choose(flag, first[...], second[...])
        tables[n, :, rows:] = choose(flag, second[...], first[...])

    if round_index == 0:
        near, far = table_refs[:4], table_refs[4:]

        @pl.when(core == 0)
        def _():
            lay(0, low, near[0], near[1])
            lay(1, low, near[2], near[3])
            lay(2, y, far[2], far[3])

        @pl.when(core == 1)
        def _():
            lay(0, low, far[0], far[1])
            lay(1, low, far[2], far[3])
            lay(2, y, near[0], near[1])
    else:
        for n, first in ((0, 0), (1, 2), (2, 2), (3, 0)):
            lay(n, y, table_refs[first], table_refs[first + 1])

    def packed_of(n, pair):
        return jnp.concatenate([lists[n, pair, k : k + 1, :] for k in range(2)], 1)

    def kinds_of(n, pair):
        return jnp.concatenate([lists[n, pair, 3 + k : 4 + k, :] for k in range(2)], 1)

    def one_hot(size, ids):
        row_ids = lax.broadcasted_iota(jnp.int16, (size, ids.shape[1]), 0)
        ids = jnp.where(jnp.logical_and(ids >= 0, ids < size), ids, -1).astype(jnp.int16)
        return jnp.where(row_ids == ids, jnp.ones((), BF16), jnp.zeros((), BF16))

    def relate_of(kinds):
        chosen = one_hot(relations_ref.shape[1], kinds)
        return jnp.dot(relations_ref[...], chosen, preferred_element_type=F32)

    span = pairs * LANES

    def side_ids(n, k):
        packed = [lists[n, pair, k : k + 1, :] for pair in range(pairs)]
        return jnp.bitwise_and(jnp.concatenate(packed, 1), 65535)

    lane = lax.broadcasted_iota(I32, (1, LANES), 1)
    notes = jnp.zeros((1, LANES), I32)
    for n in range(total):
        for pair in range(pairs):
            left, right, late = (
                jnp.bitwise_and(lists[n, pair, row : row + 1, :], 65535) for row in range(3)
            )
            over = jnp.logical_and(left >= rows, left < NOBODY)
            for bit, lane_at, there in (
                (2 * n, LANES - 1, over),
                (2 * n + 1, 0, right < rows),
                (8 + 4 * n + pair, 0, late < NOBODY),
            ):
                there = jnp.logical_and(there, lane == lane_at)
                notes = jnp.bitwise_or(notes, jnp.where(there, 1 << bit, 0))
    notes = jnp.sum(notes)
    crossed = [
        [jnp.bitwise_and(notes, 1 << (2 * n + k)) != 0 for k in range(2)] for n in range(total)
    ]
    for n in range(total):
        for k in range(2):
            pick = one_hot(rows, side_ids(n, k) - k * rows)
            picks[n, k] = pick
            values[n, :, k * span : (k + 1) * span] = jnp.dot(
                tables[n, :, k * rows : (k + 1) * rows], pick, preferred_element_type=F32
            ).astype(BF16)
    for n in range(total):
        for k in range(2):

            @pl.when(crossed[n][k])
            def _():
                pick = one_hot(rows, side_ids(n, k) - (1 - k) * rows)
                values[n, :, k * span : (k + 1) * span] += jnp.dot(
                    tables[n, :, (1 - k) * rows : (2 - k) * rows], pick, preferred_element_type=F32
                ).astype(BF16)

    def compute(pair, sources, targets):
        cuts = [slice(k * span + pair * LANES, k * span + (pair + 1) * LANES) for k in range(2)]

        def joined(chosen, get):
            return jnp.concatenate([get(n) for n in chosen], 1)

        def rows_of(chosen):
            return jnp.concatenate([values[n, :, cut] for n in chosen for cut in cuts], 1)

        def edges(chosen):
            return joined(chosen, lambda n: jnp.right_shift(packed_of(n, pair), 16))

        got = tile(
            rows_of(sources),
            rows_of(targets),
            relate_of(joined(sources, lambda n: kinds_of(n, pair))),
            edges(sources),
            edges(targets),
        )
        for chosen, grads in zip((sources, targets), got):
            for at, (n, cut) in enumerate((n, cut) for n in chosen for cut in cuts):
                values[n, :, cut] = grads[:, at * LANES : (at + 1) * LANES]

    if round_index == 0:

        @pl.when(core == 0)
        def _():
            for pair in range(pairs):
                compute(pair, (0, 1), (2,))

        @pl.when(core == 1)
        def _():
            for pair in range(pairs):
                compute(pair, (2,), (0, 1))
    else:
        for pair in range(pairs):
            compute(pair, (0,), (1,))
            compute(pair, (2,), (3,))

    def scatter(grads, pick):
        return lax.dot_general(grads, pick, (((1,), (1,)), ((), ())), preferred_element_type=F32)

    for n in range(total):
        for k in range(2):
            sums[n, :, k * rows : (k + 1) * rows] = scatter(
                values[n, :, k * span : (k + 1) * span], picks[n, k]
            )
    for n in range(total):
        for k in range(2):

            @pl.when(crossed[n][k])
            def _():
                pick = one_hot(rows, side_ids(n, k) - (1 - k) * rows)
                sums[n, :, (1 - k) * rows : (2 - k) * rows] += scatter(
                    values[n, :, k * span : (k + 1) * span], pick
                )

    @pl.when(jnp.right_shift(notes, 8) != 0)
    def _():
        spare = jnp.full((1, LANES), NOBODY, I32)

        def each(step, carry):
            pair, task = step // 2, step % 2
            if round_index == 0:
                chosen = (jnp.where(core == 0, task, 2), jnp.where(core == 0, 2, task))
            else:
                chosen = (2 * task, 2 * task + 1)
            has_late = [
                jnp.bitwise_and(jnp.right_shift(notes, 8 + 4 * chosen[side] + pair), 1)
                for side in range(2)
            ]

            def combine(combo, carry):
                late = (jnp.where(combo != 1, 1, 0), jnp.where(combo != 0, 1, 0))

                @pl.when(jnp.logical_and(has_late[0] >= late[0], has_late[1] >= late[1]))
                def _():
                    found = []
                    for side in range(2):

                        def rows_of(first, side=side):
                            left, right, extra = (
                                lists[chosen[side], pair, first + row : first + row + 1, :]
                                for row in range(3)
                            )
                            return jnp.where(
                                late[side] == 0,
                                jnp.concatenate([left, right], 1),
                                jnp.concatenate([extra, spare], 1),
                            )

                        packed = rows_of(0)
                        pick = one_hot(2 * rows, jnp.bitwise_and(packed, 65535))
                        gathered = jnp.dot(
                            tables[chosen[side]], pick, preferred_element_type=F32
                        ).astype(BF16)
                        found.append((gathered, pick, jnp.right_shift(packed, 16), rows_of))
                    grads = tile(
                        found[0][0],
                        found[1][0],
                        relate_of(found[0][3](3)),
                        found[0][2],
                        found[1][2],
                    )
                    for side in range(2):
                        sums[chosen[side]] += scatter(grads[side], found[side][1])

                return carry

            @pl.when(has_late[0] + has_late[1] > 0)
            def _():
                lax.fori_loop(0, 3, combine, 0)

            return carry

        lax.fori_loop(0, pairs * 2, each, 0)

    def part(total, which):
        return choose(which, total[:, :rows], total[:, rows:])

    if round_index > 0:
        near = sums[0] + sums[3]
        far = sums[1] + sums[2]
        out_refs[0][...] = part(near, y)
        out_refs[1][...] = part(near, 1 - y).astype(BF16)
        out_refs[2][...] = part(far, y).astype(BF16)
        out_refs[3][...] = part(far, 1 - y).astype(BF16)
        return

    def put(outs, n, which):
        for k in range(2):
            outs[k][...] = part(sums[n], which if k == 0 else 1 - which).astype(outs[k].dtype)

    def clear(outs):
        for ref in outs:
            ref[...] = jnp.zeros(ref.shape, ref.dtype)

    @pl.when(core == 0)
    def _():
        put(out_refs[0:2], 0, low)
        put(out_refs[2:4], 1, low)
        clear(out_refs[4:6])
        put(out_refs[6:8], 2, y)

    @pl.when(core == 1)
    def _():
        put(out_refs[0:2], 2, y)
        clear(out_refs[2:4])
        put(out_refs[4:6], 0, low)
        put(out_refs[6:8], 1, low)


def tiles(round_index, lists, relations, tables):
    padded, rows = tables[0].shape
    total, pairs = lists.shape[:2]

    def kernel(*refs):
        tiles_kernel(round_index, *refs)

    kinds = [F32] * 4 + [BF16] * 4 if round_index == 0 else [F32] + [BF16] * 3
    operands = (lists, relations, *tables)
    return pl.pallas_call(
        kernel,
        out_shape=tuple(jax.ShapeDtypeStruct((padded, rows), kind) for kind in kinds),
        in_specs=[VMEM] * len(operands),
        out_specs=(VMEM,) * len(kinds),
        scratch_shapes=[
            pltpu.VMEM((total, padded, 2 * rows), BF16),
            pltpu.VMEM((total, 2, rows, pairs * LANES), BF16),
            pltpu.VMEM((total, padded, pairs * CHUNK), BF16),
            pltpu.VMEM((total, padded, 2 * rows), F32),
        ],
        compiler_params=PARAMS,
        cost_estimate=pl.CostEstimate(
            flops=8_000_000_000, bytes_accessed=8_000_000, transcendentals=1_000_000
        ),
        name="tiles",
    )(*operands)


def update_kernel(master_ref, state_ref, own_ref, a_ref, b_ref, c_ref, *outs):
    width = master_ref.shape[0]
    half, padded = halves(width)
    gradient = (own_ref[...] + a_ref[...].astype(F32)) + (
        b_ref[...].astype(F32) + c_ref[...].astype(F32)
    )
    gradient = jnp.concatenate([gradient[:half], gradient[padded : padded + half]], 0)
    state = state_ref[...] + jnp.sum(gradient * gradient, axis=0, keepdims=True) / width
    master = master_ref[...] - gradient * (learn_rate / jnp.sqrt(state))
    outs[0][...] = master
    outs[1][...] = state
    if len(outs) > 2:
        outs[2][...] = spread(master, padded).astype(BF16)


def update(master, state, own, a, b, c, last):
    shapes = [(master.shape, F32), (state.shape, F32)]
    if not last:
        shapes.append((own.shape, BF16))
    return pl.pallas_call(
        update_kernel,
        out_shape=tuple(jax.ShapeDtypeStruct(*shape) for shape in shapes),
        in_specs=[VMEM] * 6,
        out_specs=(VMEM,) * len(shapes),
        compiler_params=PARAMS,
        name="update",
    )(master, state, own, a, b, c)


def tile_body(entity_table, adagrad_state, relations, sources, targets, relation_ids, edge_counts):
    rows = entity_table.shape[1]
    entity = entity_table[0].T
    state = adagrad_state
    row_total = lax.axis_size("row")
    wire, ids = open_tables(entity, edge_counts, sources, targets, relation_ids, row_total)
    ids = lax.all_to_all(ids, "row", split_axis=0, concat_axis=0, tiled=True)
    near = [wire, None] + [move(wire, pairs) for pairs in FIRST[1:]]
    tied_wire, _ = lax.optimization_barrier((wire, ids))
    near[1] = move(tied_wire, FIRST[0])
    near[2], near[3], ids = lax.optimization_barrier((near[2], near[3], ids))
    lists, relate = make_lists(0, [ids], relations, rows)
    other_ids = move(ids, SWAP_X)
    far = [move(block, SWAP_CORE) for block in near]

    outs = tiles(0, lists, relate, near + far)
    outs, ids, other_ids = lax.optimization_barrier((outs, ids, other_ids))
    cross = [move(block, SWAP_CORE).astype(F32) for block in outs[4:]]
    sent = [(outs[1 + k] + cross[1 + k]).astype(BF16) for k in range(3)]
    parts = [move(sent[k], back(FIRST[k])) for k in range(3)]
    own, ids, other_ids, _ = lax.optimization_barrier((outs[0] + cross[0], ids, other_ids, sent))
    (lists,) = make_lists(1, [ids, other_ids], relations, rows)
    entity, lists = lax.optimization_barrier((entity, lists))
    entity, state, wire = update(entity, state, own, *parts, False)

    near = [wire] + [move(wire, pairs) for pairs in SECOND]
    own, *parts = tiles(1, lists, relate, near)
    parts = [move(parts[k], back(SECOND[k])) for k in range(3)]
    entity, state = update(entity, state, own, *parts, True)
    return (entity.T[None], state)


def shifted(value, axis, steps):
    count = lax.axis_size(axis)
    pairs = [(source, (source + steps) % count) for source in range(count)]
    return lax.ppermute(value, axis, pairs)


def edge_grads(src_rows, dst_rows, rel_rows, live_mask):
    half_width = src_rows.shape[-1] // 2
    source = src_rows.astype(jnp.float32)
    relate = rel_rows.astype(jnp.float32)
    src_real = source[..., :half_width]
    src_imag = source[..., half_width:]
    rel_real = relate[..., :half_width]
    rel_imag = relate[..., half_width:]
    queries = jnp.concatenate(
        [src_real * rel_real - src_imag * rel_imag, src_real * rel_imag + src_imag * rel_real], -1
    ).astype(jnp.bfloat16)
    scores = jnp.einsum("bik,bjk->bij", queries, dst_rows, preferred_element_type=jnp.float32)
    block_size = scores.shape[-1]
    diagonal = jnp.arange(block_size)[:, None] == jnp.arange(block_size)[None, :]
    pair_mask = live_mask[:, :, None] * live_mask[:, None, :]
    weights = (
        jnp.where(diagonal, -jax.nn.sigmoid(-scores), jax.nn.sigmoid(scores) / block_size)
        * pair_mask
    ).astype(jnp.bfloat16)
    query_grad = jnp.einsum("bij,bjk->bik", weights, dst_rows, preferred_element_type=jnp.float32)
    dst_grad = jnp.einsum("bij,bik->bjk", weights, queries, preferred_element_type=jnp.float32)
    grad_real = query_grad[..., :half_width]
    grad_imag = query_grad[..., half_width:]
    src_grad = jnp.concatenate(
        [grad_real * rel_real + grad_imag * rel_imag, grad_imag * rel_real - grad_real * rel_imag],
        -1,
    )
    return (src_grad.astype(jnp.bfloat16), dst_grad.astype(jnp.bfloat16))


def slot_places(row_ids, rows_per, holders_total, capacity):
    holder = row_ids // rows_per
    onehot = (holder[:, None] == jnp.arange(holders_total)[None, :]).astype(jnp.int32)
    running = jnp.cumsum(onehot, axis=0)
    rank = jnp.sum(onehot * running, axis=-1) - 1
    place = holder * capacity + rank
    request = (
        jnp.zeros((holders_total * capacity,), jnp.int32).at[place].set(row_ids - holder * rows_per)
    )
    return (place, request.reshape(holders_total, capacity))


def plain_body(entity_table, adagrad_state, relations, sources, targets, relation_ids, edge_counts):
    entity = entity_table[0]
    adagrad = adagrad_state[0]
    rows_per = entity.shape[0]
    width = entity.shape[1]
    slot_total = sources.shape[-1]
    holders_total = lax.axis_size("row")
    capacity = 2 * slot_total // holders_total
    slot_ids = jnp.arange(slot_total)
    rel_columns = jnp.arange(relations.shape[0])
    for round_index in range(ROUNDS):
        shift_by = round_index + 1
        src_ids = sources[round_index, 0]
        dst_ids = targets[round_index, 0]
        live_total = edge_counts[round_index, 0, 0]
        live_mask = (slot_ids < live_total).astype(jnp.float32)
        rel_onehot = (relation_ids[round_index, 0][:, None] == rel_columns[None, :]).astype(
            jnp.bfloat16
        )
        rel_rows = jnp.dot(rel_onehot, relations, preferred_element_type=jnp.float32).astype(
            jnp.bfloat16
        )
        own_rows = entity.astype(jnp.bfloat16)
        src_place, src_request = slot_places(src_ids, rows_per, holders_total, capacity)
        dst_place, dst_request = slot_places(dst_ids, rows_per, holders_total, capacity)
        serve_table = shifted(own_rows, "dom", shift_by)
        wanted = (
            lax.all_to_all(src_request, "row", split_axis=0, concat_axis=0, tiled=True),
            lax.all_to_all(dst_request, "row", split_axis=0, concat_axis=0, tiled=True),
        )
        src_serve = jnp.take(own_rows, wanted[0].reshape(-1), axis=0).reshape(
            holders_total, capacity, width
        )
        dst_serve = jnp.take(serve_table, wanted[1].reshape(-1), axis=0).reshape(
            holders_total, capacity, width
        )
        answered = (
            lax.all_to_all(src_serve, "row", split_axis=0, concat_axis=0, tiled=True),
            lax.all_to_all(dst_serve, "row", split_axis=0, concat_axis=0, tiled=True),
        )
        dst_answer = answered[1]
        src_rows = jnp.take(answered[0].reshape(-1, width), src_place, axis=0)
        dst_rows = jnp.take(dst_answer.reshape(-1, width), dst_place, axis=0)
        src_grad, dst_grad = edge_grads(
            src_rows.reshape(-1, GROUP, width),
            dst_rows.reshape(-1, GROUP, width),
            rel_rows.reshape(-1, GROUP, width),
            live_mask.reshape(-1, GROUP),
        )
        src_grad = src_grad.reshape(slot_total, width)
        dst_grad = dst_grad.reshape(slot_total, width)
        blank = jnp.zeros((holders_total * capacity, width), jnp.bfloat16)
        src_buffer = blank.at[src_place].set(src_grad).reshape(holders_total, capacity, width)
        dst_buffer = blank.at[dst_place].set(dst_grad).reshape(holders_total, capacity, width)
        parts = (
            lax.all_to_all(src_buffer, "row", split_axis=0, concat_axis=0, tiled=True),
            lax.all_to_all(dst_buffer, "row", split_axis=0, concat_axis=0, tiled=True),
        )
        lhs_sum = jax.ops.segment_sum(
            parts[0].reshape(-1, width).astype(jnp.float32),
            wanted[0].reshape(-1),
            num_segments=rows_per,
        )
        other_sum = jax.ops.segment_sum(
            parts[1].reshape(-1, width).astype(jnp.float32),
            wanted[1].reshape(-1),
            num_segments=rows_per,
        )
        returned = shifted(other_sum, "dom", -shift_by)
        gradient = lhs_sum + returned
        adagrad = adagrad + jnp.mean(gradient * gradient, axis=-1)
        entity = entity - learn_rate * gradient / jnp.sqrt(adagrad)[:, None]
    return (entity[None], adagrad[None])


def solution(mesh):
    in_specs = (
        P("dom", "row", None),
        P("dom", "row"),
        P(),
        P(None, "dom", "row"),
        P(None, "dom", "row"),
        P(None, "dom", "row"),
        P(None, "dom", "row"),
    )
    out_specs = (P("dom", "row", None), P("dom", "row"))

    def body(entity_table, adagrad_state, relations, sources, *rest):
        fits = (
            (mesh.shape["dom"], mesh.shape["row"]) == (4, 8)
            and entity_table.shape[1] == 256
            and sources.shape[-1] == GROUP
        )
        chosen = tile_body if fits else plain_body
        return chosen(entity_table, adagrad_state, relations, sources, *rest)

    return jax.shard_map(body, mesh=mesh, in_specs=in_specs, out_specs=out_specs, check_vma=False)
```

```python
import jax
import jax.numpy as jnp
from jax import lax
from jax.experimental import pallas as pl
from jax.experimental.pallas import tpu as pltpu
from jax.sharding import PartitionSpec as P

GROUP = 384
ROUNDS = 2
LANES = 128
CHUNK = 2 * LANES
NOBODY = 65535
DEAD = 32767

learn_rate = 0.1

F32 = jnp.float32
BF16 = jnp.bfloat16
I32 = jnp.int32
VMEM = pl.BlockSpec(memory_space=pltpu.VMEM)
HBM = pl.BlockSpec(memory_space=pltpu.HBM)
PARAMS = pltpu.CompilerParams(vmem_limit_bytes=48 * 1024 * 1024)


def place(x, core, z, y):
    return (x * 2 + core) * 8 + z * 2 + y


PLACES = [(x, c, z, y) for x in range(2) for c in range(2) for z in range(4) for y in range(2)]


def route(target):
    return [(place(*at), place(*target(*at))) for at in PLACES]


def far_z(x, z, y):
    swap = (z & 1) ^ (z >> 1) ^ y
    return z ^ (3 * swap * (1 - x) + (1 + swap) * x)


FIRST = [
    route(lambda x, c, z, y: (x, c, z ^ 1, y) if c == 0 else (x, c, z, y ^ 1)),
    route(lambda x, c, z, y: (x, c, z ^ 2, y) if c == 0 else (x ^ 1, c, z, y)),
    route(lambda x, c, z, y: (x, c, z ^ 3, y) if c == 0 else (x ^ 1, c, z, y ^ 1)),
]
SWAP_CORE = route(lambda x, c, z, y: (x, c ^ 1, z, y))
SWAP_X = route(lambda x, c, z, y: (x ^ 1, c, z, y))
SWAP_Y = route(lambda x, c, z, y: (x, c, z, y ^ 1))
SECOND = [
    SWAP_Y,
    [(place(x ^ 1, c, far_z(x, z, y), y), place(x, c, z, y)) for x, c, z, y in PLACES],
    [(place(x ^ 1, c, far_z(x, z, y), y ^ 1), place(x, c, z, y)) for x, c, z, y in PLACES],
]


def move(value, pairs):
    return lax.ppermute(value, ("dom", "row"), pairs)


def back(pairs):
    return [(target, source) for source, target in pairs]


def here():
    dom = lax.axis_index("dom")
    row = lax.axis_index("row")
    return dom // 2, dom % 2, row // 2, row % 2


def open_kernel(
    entity_ref, count_ref, source_ref, target_ref, relation_ref, wire_ref, ids_ref, *scratch
):
    entity, counts, slots, sem = scratch
    refs = (source_ref, target_ref, relation_ref)
    copies = [pltpu.make_async_copy(refs[n], slots.at[n], sem.at[n]) for n in range(3)]
    copies.append(pltpu.make_async_copy(count_ref, counts, sem.at[3]))
    copies.append(pltpu.make_async_copy(entity_ref, entity, sem.at[4]))
    for copy in copies:
        copy.start()
    for copy in copies:
        copy.wait()
    wire_ref[...] = entity[...].astype(BF16)
    edge = lax.broadcasted_iota(I32, (1, ids_ref.shape[2]), 1)
    rows, kinds = [], []
    for round_index in range(ROUNDS):
        live = edge < counts[0:1, round_index : round_index + 1]
        source = jnp.where(live, slots[0, round_index], DEAD)
        target = jnp.where(live, slots[1, round_index], DEAD)
        rows.append(jnp.bitwise_or(source, jnp.left_shift(target, 16)))
        kinds.append(slots[2, round_index])
    rows.append(jnp.bitwise_or(kinds[0], jnp.left_shift(kinds[1], 16)))
    ids = jnp.concatenate(rows + [jnp.zeros_like(edge)], 0)
    for n in range(ids_ref.shape[0]):
        ids_ref[n] = ids


def open_tables(entity, edge_counts, sources, targets, relation_ids, copies):
    width, rows = entity.shape
    slots = sources.shape[-1]
    return pl.pallas_call(
        open_kernel,
        out_shape=(
            jax.ShapeDtypeStruct((width, rows), BF16),
            jax.ShapeDtypeStruct((copies, 4, slots), I32),
        ),
        in_specs=[HBM] * 5,
        out_specs=(VMEM, VMEM),
        scratch_shapes=[
            pltpu.VMEM((width, rows), F32),
            pltpu.VMEM((1, ROUNDS), I32),
            pltpu.VMEM((3, ROUNDS, 1, slots), I32),
            pltpu.SemaphoreType.DMA((5,)),
        ],
        name="open_tables",
    )(entity, edge_counts.reshape(1, ROUNDS), sources, targets, relation_ids)


def wanted_lists(round_index):
    x, core, z, y = here()
    if round_index == 0:
        line = z // 2 * 2 + y
        other_line = (1 - z // 2) * 2 + y
        return [(0, core, line), (0, core, other_line), (0, 1 - core, z)]
    swap = (z % 2 + z // 2 + y) % 2
    far = jnp.bitwise_xor(z, jnp.where(x == 0, 3 * swap, 1 + swap))
    return [(0, 0, z), (0, 1, far), (1, 0, far), (1, 1, z)]


def lists_kernel(round_index, rows_per, *refs):
    buckets = 1 if round_index == 0 else 2
    id_refs, (relations_ref, out_ref, *relate_ref) = refs[:buckets], refs[buckets:]
    blocks, _, slots = id_refs[0].shape
    pairs = blocks // 2
    lists = wanted_lists(round_index)
    if relate_ref:
        width = relations_ref.shape[1]
        full = -(-width // LANES) * LANES
        relations = jnp.pad(relations_ref[...].astype(F32), ((0, 0), (0, full - width)))
        relate_ref[0][...] = relations.T[:width].astype(BF16)
    lower = lax.broadcasted_iota(I32, (slots, slots), 0)
    upper = lax.broadcasted_iota(I32, (slots, slots), 1)
    before = (lower <= upper).astype(F32).astype(BF16)
    edge = lax.broadcasted_iota(I32, (1, slots), 1)
    one = jnp.ones_like(edge)
    order = [(n, pair) for n in range(len(lists)) for pair in range(pairs)]

    values, masks = [], []
    for ref in id_refs:
        packed = jnp.concatenate([ref[b, round_index : round_index + 1, :] for b in range(blocks)], 0)
        kinds = jnp.concatenate([ref[b, 2:3, :] for b in range(blocks)], 0)
        kinds = jnp.bitwise_and(jnp.right_shift(kinds, 16 * round_index), 65535)
        sides = [jnp.bitwise_and(packed, 65535), jnp.right_shift(packed, 16)]
        values.append((sides, kinds))
    spots = []
    for bucket, side, group in lists:
        sides, kinds = values[bucket]
        if round_index == 0:
            ids = jnp.where(side == 0, sides[0], sides[1])
        else:
            ids = sides[side]
        live = sides[0] != DEAD
        holder = ids // rows_per
        local = jnp.where(live, ids - holder * rows_per, 0)
        if round_index == 0 and len(spots) < 2:
            mine = holder // 4 * 2 + holder % 2 == group
            which = holder // 2 % 2
        else:
            mine = holder // 2 == group
            which = holder % 2
        mine = jnp.logical_and(mine, live)
        spots.append((local, jnp.where(live, which, 0), mine, kinds))
        for k in range(2):
            masks.append(jnp.logical_and(mine, which == k).astype(F32))
    stacked = jnp.concatenate(masks, 0).astype(BF16)
    running = jnp.dot(stacked, before, preferred_element_type=F32)
    slots_of, late = [], []
    for n, (local, which, mine, kinds) in enumerate(spots):
        even, odd = (
            running[(2 * n + k) * blocks : (2 * n + k + 1) * blocks] for k in range(2)
        )
        second = lax.broadcasted_iota(I32, (blocks, 1), 0) % 2 == 1
        totals = [part[:, slots - 1 : slots] for part in (even, odd)]
        ahead = [
            jnp.concatenate([total[:1], total[:-1]], 0) for total in totals
        ]
        behind = [jnp.concatenate([total[1:], total[:1]], 0) for total in totals]
        whole = [
            total + jnp.where(second, a, b) for total, a, b in zip(totals, ahead, behind)
        ]
        even = even + jnp.where(second, ahead[0], 0.0)
        odd = odd + jnp.where(second, ahead[1], 0.0)
        room = CHUNK - whole[1]
        slot = jnp.where(
            which == 1, CHUNK - odd, jnp.where(even <= room, even - 1, CHUNK + even - 1 - room)
        )
        slots_of.append(jnp.where(mine, slot, -1.0))
        bit = lax.broadcasted_iota(I32, (blocks, 1), 0) // 2 + pairs * n
        over = jnp.logical_and(jnp.logical_not(second), whole[0] > room)
        late.append(jnp.where(over, jnp.left_shift(jnp.ones_like(bit), bit), 0))
    late = jnp.sum(jnp.concatenate(late, 0))
    chunk_ids = lax.broadcasted_iota(I32, (CHUNK, 2 * slots), 0).astype(F32)
    late_ids = lax.broadcasted_iota(I32, (LANES, 2 * slots), 0).astype(F32) + CHUNK
    edges = jnp.concatenate([edge, edge + slots], 1)
    nobody = jnp.full((1, LANES), NOBODY, I32)
    blank = jnp.zeros((1, LANES), I32)
    for n, (local, which, mine, kinds) in enumerate(spots):
        for pair in range(pairs):

            def joined(part, pair=pair):
                return jnp.concatenate([part[2 * pair : 2 * pair + 1], part[2 * pair + 1 : 2 * pair + 2]], 1)

            slot = joined(slots_of[n])
            columns = (
                jnp.concatenate(
                    [
                        joined(local),
                        joined(which),
                        joined(kinds),
                        edges // 32,
                        edges % 32,
                        jnp.ones_like(edges),
                    ]
                    + [jnp.zeros_like(edges)] * 2,
                    0,
                )
                .astype(F32)
                .astype(BF16)
            )

            def rows_at(slot_ids, slot=slot, columns=columns):
                chosen = (slot_ids == slot).astype(F32).astype(BF16)
                got = lax.dot_general(
                    columns, chosen, (((1,), (1,)), ((), ())), preferred_element_type=F32
                ).astype(I32)
                ids = jnp.where(got[5:6] > 0, got[1:2] * rows_per + got[0:1], NOBODY)
                return jnp.bitwise_or(ids, jnp.left_shift(got[3:4] * 32 + got[4:5], 16)), got[2:3]

            packed, kind = rows_at(chunk_ids)
            for k in range(2):
                cut = slice(k * LANES, (k + 1) * LANES)
                out_ref[n, pair, k : k + 1, :] = packed[:, cut]
                out_ref[n, pair, 3 + k : 4 + k, :] = kind[:, cut]
            out_ref[n, pair, 2:3, :] = nobody
            out_ref[n, pair, 5:6, :] = blank

            @pl.when(jnp.bitwise_and(jnp.right_shift(late, pairs * n + pair), 1) > 0)
            def _():
                packed, kind = rows_at(late_ids)
                out_ref[n, pair, 2:3, :] = packed
                out_ref[n, pair, 5:6, :] = kind


def make_lists(round_index, ids, relations, rows_per):
    width = relations.shape[1]

    def kernel(*refs):
        lists_kernel(round_index, rows_per, *refs)

    shapes = [jax.ShapeDtypeStruct((3 + round_index, ids[0].shape[0] // 2, 8, LANES), I32)]
    if round_index == 0:
        shapes.append(jax.ShapeDtypeStruct((width, relations.shape[0]), BF16))
    return pl.pallas_call(
        kernel,
        out_shape=tuple(shapes),
        in_specs=[VMEM] * (len(ids) + 1),
        out_specs=(VMEM,) * len(shapes),
        compiler_params=PARAMS,
        cost_estimate=pl.CostEstimate(
            flops=4_000_000_000, bytes_accessed=1_000_000, transcendentals=0
        ),
        name="make_lists",
    )(*ids, relations)


def both(left, right):
    return jnp.concatenate([left, right], 0)


def tile(source, target, relate, source_edge, target_edge):
    half = source.shape[0] // 2
    relate_re, relate_im = relate[:half], relate[half:]
    source = source.astype(F32)
    source_re, source_im = source[:half], source[half:]
    queries = both(
        source_re * relate_re - source_im * relate_im,
        source_re * relate_im + source_im * relate_re,
    ).astype(BF16)
    scores = lax.dot_general(
        queries, target, (((0,), (0,)), ((), ())), preferred_element_type=F32
    )
    edge_row = target_edge.astype(F32)
    edge_col = jnp.broadcast_to(source_edge.astype(F32), (8, source_edge.shape[1])).T[:, :1]
    bent = 0.5 * jnp.tanh(0.5 * scores)
    weights = jnp.where(
        edge_col == edge_row,
        bent - 0.5,
        jnp.where((edge_col < GROUP) == (edge_row < GROUP), (bent + 0.5) * (1.0 / GROUP), 0.0),
    ).astype(BF16)
    query_grad = lax.dot_general(
        target, weights, (((1,), (1,)), ((), ())), preferred_element_type=F32
    )
    target_grad = jnp.dot(queries, weights, preferred_element_type=F32).astype(BF16)
    grad_re, grad_im = query_grad[:half], query_grad[half:]
    source_grad = both(
        grad_re * relate_re + grad_im * relate_im,
        grad_im * relate_re - grad_re * relate_im,
    ).astype(BF16)
    return source_grad, target_grad


def tiles_kernel(round_index, *refs):
    lists, relations_ref, refs = refs[0], refs[1], refs[2:]
    count = 8 if round_index == 0 else 4
    table_refs, out_refs = refs[:count], refs[count : 2 * count]
    tables, picks, values, sums = refs[2 * count :]
    padded, rows = table_refs[0].shape
    total, pairs = lists.shape[:2]
    x, core, z, y = here()
    low = z % 2

    def choose(flag, first, second):
        return jnp.where(flag == 0, first, second)

    def lay(n, flag, first, second):
        tables[n, :, :rows] = choose(flag, first[...], second[...])
        tables[n, :, rows:] = choose(flag, second[...], first[...])

    if round_index == 0:
        near, far = table_refs[:4], table_refs[4:]

        @pl.when(core == 0)
        def _():
            lay(0, low, near[0], near[1])
            lay(1, low, near[2], near[3])
            lay(2, y, far[2], far[3])

        @pl.when(core == 1)
        def _():
            lay(0, low, far[0], far[1])
            lay(1, low, far[2], far[3])
            lay(2, y, near[0], near[1])
    else:
        for n, first in ((0, 0), (1, 2), (2, 2), (3, 0)):
            lay(n, y, table_refs[first], table_refs[first + 1])

    def packed_of(n, pair):
        return jnp.concatenate([lists[n, pair, k : k + 1, :] for k in range(2)], 1)

    def kinds_of(n, pair):
        return jnp.concatenate([lists[n, pair, 3 + k : 4 + k, :] for k in range(2)], 1)

    def one_hot(size, ids):
        row_ids = lax.broadcasted_iota(jnp.int16, (size, ids.shape[1]), 0)
        ids = jnp.where(jnp.logical_and(ids >= 0, ids < size), ids, -1).astype(jnp.int16)
        return jnp.where(row_ids == ids, jnp.ones((), BF16), jnp.zeros((), BF16))

    def relate_of(kinds):
        chosen = one_hot(relations_ref.shape[1], kinds)
        return jnp.dot(relations_ref[...], chosen, preferred_element_type=F32)

    span = pairs * LANES

    def side_ids(n, k):
        packed = [lists[n, pair, k : k + 1, :] for pair in range(pairs)]
        return jnp.bitwise_and(jnp.concatenate(packed, 1), 65535)

    lane = lax.broadcasted_iota(I32, (1, LANES), 1)
    notes = jnp.zeros((1, LANES), I32)
    for n in range(total):
        for pair in range(pairs):
            left, right, late = (
                jnp.bitwise_and(lists[n, pair, row : row + 1, :], 65535) for row in range(3)
            )
            over = jnp.logical_and(left >= rows, left < NOBODY)
            for bit, lane_at, there in (
                (2 * n, LANES - 1, over),
                (2 * n + 1, 0, right < rows),
                (8 + 4 * n + pair, 0, late < NOBODY),
            ):
                there = jnp.logical_and(there, lane == lane_at)
                notes = jnp.bitwise_or(notes, jnp.where(there, 1 << bit, 0))
    notes = jnp.sum(notes)
    crossed = [
        [jnp.bitwise_and(notes, 1 << (2 * n + k)) != 0 for k in range(2)] for n in range(total)
    ]
    for n in range(total):
        for k in range(2):
            pick = one_hot(rows, side_ids(n, k) - k * rows)
            picks[n, k] = pick
            values[n, :, k * span : (k + 1) * span] = jnp.dot(
                tables[n, :, k * rows : (k + 1) * rows], pick, preferred_element_type=F32
            ).astype(BF16)
    for n in range(total):
        for k in range(2):

            @pl.when(crossed[n][k])
            def _():
                pick = one_hot(rows, side_ids(n, k) - (1 - k) * rows)
                values[n, :, k * span : (k + 1) * span] += jnp.dot(
                    tables[n, :, (1 - k) * rows : (2 - k) * rows], pick, preferred_element_type=F32
                ).astype(BF16)

    def compute(pair, sources, targets):
        cuts = [slice(k * span + pair * LANES, k * span + (pair + 1) * LANES) for k in range(2)]

        def joined(chosen, get):
            return jnp.concatenate([get(n) for n in chosen], 1)

        def rows_of(chosen):
            return jnp.concatenate([values[n, :, cut] for n in chosen for cut in cuts], 1)

        def edges(chosen):
            return joined(chosen, lambda n: jnp.right_shift(packed_of(n, pair), 16))

        got = tile(
            rows_of(sources),
            rows_of(targets),
            relate_of(joined(sources, lambda n: kinds_of(n, pair))),
            edges(sources),
            edges(targets),
        )
        for chosen, grads in zip((sources, targets), got):
            for at, (n, cut) in enumerate((n, cut) for n in chosen for cut in cuts):
                values[n, :, cut] = grads[:, at * LANES : (at + 1) * LANES]

    if round_index == 0:

        @pl.when(core == 0)
        def _():
            for pair in range(pairs):
                compute(pair, (0, 1), (2,))

        @pl.when(core == 1)
        def _():
            for pair in range(pairs):
                compute(pair, (2,), (0, 1))
    else:
        for pair in range(pairs):
            compute(pair, (0,), (1,))
            compute(pair, (2,), (3,))

    def scatter(grads, pick):
        return lax.dot_general(grads, pick, (((1,), (1,)), ((), ())), preferred_element_type=F32)

    for n in range(total):
        for k in range(2):
            sums[n, :, k * rows : (k + 1) * rows] = scatter(
                values[n, :, k * span : (k + 1) * span], picks[n, k]
            )
    for n in range(total):
        for k in range(2):

            @pl.when(crossed[n][k])
            def _():
                pick = one_hot(rows, side_ids(n, k) - (1 - k) * rows)
                sums[n, :, (1 - k) * rows : (2 - k) * rows] += scatter(
                    values[n, :, k * span : (k + 1) * span], pick
                )

    @pl.when(jnp.right_shift(notes, 8) != 0)
    def _():
        spare = jnp.full((1, LANES), NOBODY, I32)

        def each(step, carry):
            pair, task = step // 2, step % 2
            if round_index == 0:
                chosen = (jnp.where(core == 0, task, 2), jnp.where(core == 0, 2, task))
            else:
                chosen = (2 * task, 2 * task + 1)
            has_late = [
                jnp.bitwise_and(jnp.right_shift(notes, 8 + 4 * chosen[side] + pair), 1)
                for side in range(2)
            ]

            def combine(combo, carry):
                late = (jnp.where(combo != 1, 1, 0), jnp.where(combo != 0, 1, 0))

                @pl.when(jnp.logical_and(has_late[0] >= late[0], has_late[1] >= late[1]))
                def _():
                    found = []
                    for side in range(2):

                        def rows_of(first, side=side):
                            left, right, extra = (
                                lists[chosen[side], pair, first + row : first + row + 1, :]
                                for row in range(3)
                            )
                            return jnp.where(
                                late[side] == 0,
                                jnp.concatenate([left, right], 1),
                                jnp.concatenate([extra, spare], 1),
                            )

                        packed = rows_of(0)
                        pick = one_hot(2 * rows, jnp.bitwise_and(packed, 65535))
                        gathered = jnp.dot(
                            tables[chosen[side]], pick, preferred_element_type=F32
                        ).astype(BF16)
                        found.append((gathered, pick, jnp.right_shift(packed, 16), rows_of))
                    grads = tile(
                        found[0][0],
                        found[1][0],
                        relate_of(found[0][3](3)),
                        found[0][2],
                        found[1][2],
                    )
                    for side in range(2):
                        sums[chosen[side]] += scatter(grads[side], found[side][1])

                return carry

            @pl.when(has_late[0] + has_late[1] > 0)
            def _():
                lax.fori_loop(0, 3, combine, 0)

            return carry

        lax.fori_loop(0, pairs * 2, each, 0)

    def part(total, which):
        return choose(which, total[:, :rows], total[:, rows:])

    if round_index > 0:
        near = sums[0] + sums[3]
        far = sums[1] + sums[2]
        out_refs[0][...] = part(near, y)
        out_refs[1][...] = part(near, 1 - y).astype(BF16)
        out_refs[2][...] = part(far, y).astype(BF16)
        out_refs[3][...] = part(far, 1 - y).astype(BF16)
        return

    def put(outs, n, which):
        for k in range(2):
            outs[k][...] = part(sums[n], which if k == 0 else 1 - which).astype(outs[k].dtype)

    def clear(outs):
        for ref in outs:
            ref[...] = jnp.zeros(ref.shape, ref.dtype)

    @pl.when(core == 0)
    def _():
        put(out_refs[0:2], 0, low)
        put(out_refs[2:4], 1, low)
        clear(out_refs[4:6])
        put(out_refs[6:8], 2, y)

    @pl.when(core == 1)
    def _():
        put(out_refs[0:2], 2, y)
        clear(out_refs[2:4])
        put(out_refs[4:6], 0, low)
        put(out_refs[6:8], 1, low)


def tiles(round_index, lists, relations, tables):
    padded, rows = tables[0].shape
    total, pairs = lists.shape[:2]

    def kernel(*refs):
        tiles_kernel(round_index, *refs)

    kinds = [F32] * 4 + [BF16] * 4 if round_index == 0 else [F32] + [BF16] * 3
    operands = (lists, relations, *tables)
    return pl.pallas_call(
        kernel,
        out_shape=tuple(jax.ShapeDtypeStruct((padded, rows), kind) for kind in kinds),
        in_specs=[VMEM] * len(operands),
        out_specs=(VMEM,) * len(kinds),
        scratch_shapes=[
            pltpu.VMEM((total, padded, 2 * rows), BF16),
            pltpu.VMEM((total, 2, rows, pairs * LANES), BF16),
            pltpu.VMEM((total, padded, pairs * CHUNK), BF16),
            pltpu.VMEM((total, padded, 2 * rows), F32),
        ],
        compiler_params=PARAMS,
        cost_estimate=pl.CostEstimate(
            flops=8_000_000_000, bytes_accessed=8_000_000, transcendentals=1_000_000
        ),
        name="tiles",
    )(*operands)


def update_kernel(master_ref, state_ref, own_ref, a_ref, b_ref, c_ref, *outs):
    gradient = (own_ref[...] + a_ref[...].astype(F32)) + (
        b_ref[...].astype(F32) + c_ref[...].astype(F32)
    )
    width = gradient.shape[0]
    state = state_ref[...] + jnp.sum(gradient * gradient, axis=0, keepdims=True) / width
    master = master_ref[...] - gradient * (learn_rate / jnp.sqrt(state))
    outs[0][...] = master
    outs[1][...] = state
    if len(outs) > 2:
        outs[2][...] = master.astype(BF16)


def update(master, state, own, a, b, c, last):
    shapes = [(master.shape, F32), (state.shape, F32)]
    if not last:
        shapes.append((master.shape, BF16))
    return pl.pallas_call(
        update_kernel,
        out_shape=tuple(jax.ShapeDtypeStruct(*shape) for shape in shapes),
        in_specs=[VMEM] * 6,
        out_specs=(VMEM,) * len(shapes),
        compiler_params=PARAMS,
        name="update",
    )(master, state, own, a, b, c)


def send(wire, routes):
    return [wire] + [move(wire, route) for route in routes]


def give_back(sums, routes):
    return [move(part, back(route)) for part, route in zip(sums, routes)]


def tile_body(entity_table, adagrad_state, relations, sources, targets, relation_ids, edge_counts):
    rows = entity_table.shape[1]
    entity = entity_table[0].T
    state = adagrad_state
    row_total = lax.axis_size("row")
    wire, ids = open_tables(entity, edge_counts, sources, targets, relation_ids, row_total)
    ids = lax.all_to_all(ids, "row", split_axis=0, concat_axis=0, tiled=True)
    near = [wire, None] + [move(wire, pairs) for pairs in FIRST[1:]]
    tied_wire, ids = lax.optimization_barrier((wire, ids))
    near[1] = move(tied_wire, FIRST[0])
    lists, relate = make_lists(0, [ids], relations, rows)
    other_ids = move(ids, SWAP_X)
    *near, lists = lax.optimization_barrier((*near, lists))
    far = [move(block, SWAP_CORE) for block in near]

    outs = tiles(0, lists, relate, near + far)
    outs, ids, other_ids = lax.optimization_barrier((outs, ids, other_ids))
    cross = [move(block, SWAP_CORE).astype(F32) for block in outs[4:]]
    sent = [(outs[1 + k] + cross[1 + k]).astype(BF16) for k in range(3)]
    parts = give_back(sent, FIRST)
    own, ids, other_ids, _ = lax.optimization_barrier((outs[0] + cross[0], ids, other_ids, sent))
    (lists,) = make_lists(1, [ids, other_ids], relations, rows)
    entity, lists = lax.optimization_barrier((entity, lists))
    entity, state, wire = update(entity, state, own, *parts, False)

    near = send(wire, SECOND)
    own, *parts = tiles(1, lists, relate, near)
    parts = give_back(parts, SECOND)
    entity, state = update(entity, state, own, *parts, True)
    return (entity.T[None], state)


def shifted(value, axis, steps):
    count = lax.axis_size(axis)
    pairs = [(source, (source + steps) % count) for source in range(count)]
    return lax.ppermute(value, axis, pairs)


def edge_grads(src_rows, dst_rows, rel_rows, live_mask):
    half_width = src_rows.shape[-1] // 2
    source = src_rows.astype(jnp.float32)
    relate = rel_rows.astype(jnp.float32)
    src_real = source[..., :half_width]
    src_imag = source[..., half_width:]
    rel_real = relate[..., :half_width]
    rel_imag = relate[..., half_width:]
    queries = jnp.concatenate(
        [src_real * rel_real - src_imag * rel_imag, src_real * rel_imag + src_imag * rel_real], -1
    ).astype(jnp.bfloat16)
    scores = jnp.einsum("bik,bjk->bij", queries, dst_rows, preferred_element_type=jnp.float32)
    block_size = scores.shape[-1]
    diagonal = jnp.arange(block_size)[:, None] == jnp.arange(block_size)[None, :]
    pair_mask = live_mask[:, :, None] * live_mask[:, None, :]
    weights = (
        jnp.where(diagonal, -jax.nn.sigmoid(-scores), jax.nn.sigmoid(scores) / block_size)
        * pair_mask
    ).astype(jnp.bfloat16)
    query_grad = jnp.einsum("bij,bjk->bik", weights, dst_rows, preferred_element_type=jnp.float32)
    dst_grad = jnp.einsum("bij,bik->bjk", weights, queries, preferred_element_type=jnp.float32)
    grad_real = query_grad[..., :half_width]
    grad_imag = query_grad[..., half_width:]
    src_grad = jnp.concatenate(
        [grad_real * rel_real + grad_imag * rel_imag, grad_imag * rel_real - grad_real * rel_imag],
        -1,
    )
    return (src_grad.astype(jnp.bfloat16), dst_grad.astype(jnp.bfloat16))


def slot_places(row_ids, rows_per, holders_total, capacity):
    holder = row_ids // rows_per
    onehot = (holder[:, None] == jnp.arange(holders_total)[None, :]).astype(jnp.int32)
    running = jnp.cumsum(onehot, axis=0)
    rank = jnp.sum(onehot * running, axis=-1) - 1
    place = holder * capacity + rank
    request = (
        jnp.zeros((holders_total * capacity,), jnp.int32).at[place].set(row_ids - holder * rows_per)
    )
    return (place, request.reshape(holders_total, capacity))


def plain_body(entity_table, adagrad_state, relations, sources, targets, relation_ids, edge_counts):
    entity = entity_table[0]
    adagrad = adagrad_state[0]
    rows_per = entity.shape[0]
    width = entity.shape[1]
    slot_total = sources.shape[-1]
    holders_total = lax.axis_size("row")
    capacity = 2 * slot_total // holders_total
    slot_ids = jnp.arange(slot_total)
    rel_columns = jnp.arange(relations.shape[0])
    for round_index in range(ROUNDS):
        shift_by = round_index + 1
        src_ids = sources[round_index, 0]
        dst_ids = targets[round_index, 0]
        live_total = edge_counts[round_index, 0, 0]
        live_mask = (slot_ids < live_total).astype(jnp.float32)
        rel_onehot = (relation_ids[round_index, 0][:, None] == rel_columns[None, :]).astype(
            jnp.bfloat16
        )
        rel_rows = jnp.dot(rel_onehot, relations, preferred_element_type=jnp.float32).astype(
            jnp.bfloat16
        )
        own_rows = entity.astype(jnp.bfloat16)
        src_place, src_request = slot_places(src_ids, rows_per, holders_total, capacity)
        dst_place, dst_request = slot_places(dst_ids, rows_per, holders_total, capacity)
        serve_table = shifted(own_rows, "dom", shift_by)
        wanted = (
            lax.all_to_all(src_request, "row", split_axis=0, concat_axis=0, tiled=True),
            lax.all_to_all(dst_request, "row", split_axis=0, concat_axis=0, tiled=True),
        )
        src_serve = jnp.take(own_rows, wanted[0].reshape(-1), axis=0).reshape(
            holders_total, capacity, width
        )
        dst_serve = jnp.take(serve_table, wanted[1].reshape(-1), axis=0).reshape(
            holders_total, capacity, width
        )
        answered = (
            lax.all_to_all(src_serve, "row", split_axis=0, concat_axis=0, tiled=True),
            lax.all_to_all(dst_serve, "row", split_axis=0, concat_axis=0, tiled=True),
        )
        dst_answer = answered[1]
        src_rows = jnp.take(answered[0].reshape(-1, width), src_place, axis=0)
        dst_rows = jnp.take(dst_answer.reshape(-1, width), dst_place, axis=0)
        src_grad, dst_grad = edge_grads(
            src_rows.reshape(-1, GROUP, width),
            dst_rows.reshape(-1, GROUP, width),
            rel_rows.reshape(-1, GROUP, width),
            live_mask.reshape(-1, GROUP),
        )
        src_grad = src_grad.reshape(slot_total, width)
        dst_grad = dst_grad.reshape(slot_total, width)
        blank = jnp.zeros((holders_total * capacity, width), jnp.bfloat16)
        src_buffer = blank.at[src_place].set(src_grad).reshape(holders_total, capacity, width)
        dst_buffer = blank.at[dst_place].set(dst_grad).reshape(holders_total, capacity, width)
        parts = (
            lax.all_to_all(src_buffer, "row", split_axis=0, concat_axis=0, tiled=True),
            lax.all_to_all(dst_buffer, "row", split_axis=0, concat_axis=0, tiled=True),
        )
        lhs_sum = jax.ops.segment_sum(
            parts[0].reshape(-1, width).astype(jnp.float32),
            wanted[0].reshape(-1),
            num_segments=rows_per,
        )
        other_sum = jax.ops.segment_sum(
            parts[1].reshape(-1, width).astype(jnp.float32),
            wanted[1].reshape(-1),
            num_segments=rows_per,
        )
        returned = shifted(other_sum, "dom", -shift_by)
        gradient = lhs_sum + returned
        adagrad = adagrad + jnp.mean(gradient * gradient, axis=-1)
        entity = entity - learn_rate * gradient / jnp.sqrt(adagrad)[:, None]
    return (entity[None], adagrad[None])


def solution(mesh):
    in_specs = (
        P("dom", "row", None),
        P("dom", "row"),
        P(),
        P(None, "dom", "row"),
        P(None, "dom", "row"),
        P(None, "dom", "row"),
        P(None, "dom", "row"),
    )
    out_specs = (P("dom", "row", None), P("dom", "row"))

    def body(entity_table, adagrad_state, relations, sources, *rest):
        fits = (
            (mesh.shape["dom"], mesh.shape["row"]) == (4, 8)
            and entity_table.shape[1] == 256
            and sources.shape[-1] == GROUP
        )
        chosen = tile_body if fits else plain_body
        return chosen(entity_table, adagrad_state, relations, sources, *rest)

    return jax.shard_map(body, mesh=mesh, in_specs=in_specs, out_specs=out_specs, check_vma=False)
```

```python
import jax
import jax.numpy as jnp
from jax import lax
from jax.experimental import pallas as pl
from jax.experimental.pallas import tpu as pltpu
from jax.sharding import PartitionSpec as P

GROUP = 384
ROUNDS = 2
LANES = 128
CHUNK = 2 * LANES
NOBODY = 65535
DEAD = 32767

learn_rate = 0.1

F32 = jnp.float32
BF16 = jnp.bfloat16
I32 = jnp.int32
VMEM = pl.BlockSpec(memory_space=pltpu.VMEM)
HBM = pl.BlockSpec(memory_space=pltpu.HBM)
PARAMS = pltpu.CompilerParams(vmem_limit_bytes=48 * 1024 * 1024)


def place(x, core, z, y):
    return (x * 2 + core) * 8 + z * 2 + y


PLACES = [(x, c, z, y) for x in range(2) for c in range(2) for z in range(4) for y in range(2)]


def route(target):
    return [(place(*at), place(*target(*at))) for at in PLACES]


def far_z(x, z, y):
    swap = (z & 1) ^ (z >> 1) ^ y
    return z ^ (3 * swap * (1 - x) + (1 + swap) * x)


FIRST = [
    route(lambda x, c, z, y: (x, c, z ^ 1, y) if c == 0 else (x, c, z, y ^ 1)),
    route(lambda x, c, z, y: (x, c, z ^ 2, y) if c == 0 else (x ^ 1, c, z, y)),
    route(lambda x, c, z, y: (x, c, z ^ 3, y) if c == 0 else (x ^ 1, c, z, y ^ 1)),
]
SWAP_CORE = route(lambda x, c, z, y: (x, c ^ 1, z, y))
SWAP_X = route(lambda x, c, z, y: (x ^ 1, c, z, y))
SWAP_Y = route(lambda x, c, z, y: (x, c, z, y ^ 1))
SECOND = [
    SWAP_Y,
    [(place(x ^ 1, c, far_z(x, z, y), y), place(x, c, z, y)) for x, c, z, y in PLACES],
    [(place(x ^ 1, c, far_z(x, z, y), y ^ 1), place(x, c, z, y)) for x, c, z, y in PLACES],
]


def move(value, pairs):
    return lax.ppermute(value, ("dom", "row"), pairs)


def back(pairs):
    return [(target, source) for source, target in pairs]


def here():
    dom = lax.axis_index("dom")
    row = lax.axis_index("row")
    return dom // 2, dom % 2, row // 2, row % 2


def open_kernel(
    entity_ref, count_ref, source_ref, target_ref, relation_ref, wire_ref, ids_ref, *scratch
):
    entity, counts, slots, sem = scratch
    refs = (source_ref, target_ref, relation_ref)
    copies = [pltpu.make_async_copy(refs[n], slots.at[n], sem.at[n]) for n in range(3)]
    copies.append(pltpu.make_async_copy(count_ref, counts, sem.at[3]))
    copies.append(pltpu.make_async_copy(entity_ref, entity, sem.at[4]))
    for copy in copies:
        copy.start()
    for copy in copies:
        copy.wait()
    wire_ref[...] = entity[...].astype(BF16)
    edge = lax.broadcasted_iota(I32, (1, ids_ref.shape[2]), 1)
    rows, kinds = [], []
    for round_index in range(ROUNDS):
        live = edge < counts[0:1, round_index : round_index + 1]
        source = jnp.where(live, slots[0, round_index], DEAD)
        target = jnp.where(live, slots[1, round_index], DEAD)
        rows.append(jnp.bitwise_or(source, jnp.left_shift(target, 16)))
        kinds.append(slots[2, round_index])
    rows.append(jnp.bitwise_or(kinds[0], jnp.left_shift(kinds[1], 16)))
    ids = jnp.concatenate(rows + [jnp.zeros_like(edge)], 0)
    for n in range(ids_ref.shape[0]):
        ids_ref[n] = ids


def open_tables(entity, edge_counts, sources, targets, relation_ids, copies):
    width, rows = entity.shape
    slots = sources.shape[-1]
    return pl.pallas_call(
        open_kernel,
        out_shape=(
            jax.ShapeDtypeStruct((width, rows), BF16),
            jax.ShapeDtypeStruct((copies, 4, slots), I32),
        ),
        in_specs=[HBM] * 5,
        out_specs=(VMEM, VMEM),
        scratch_shapes=[
            pltpu.VMEM((width, rows), F32),
            pltpu.VMEM((1, ROUNDS), I32),
            pltpu.VMEM((3, ROUNDS, 1, slots), I32),
            pltpu.SemaphoreType.DMA((5,)),
        ],
        name="open_tables",
    )(entity, edge_counts.reshape(1, ROUNDS), sources, targets, relation_ids)


def wanted_lists(round_index):
    x, core, z, y = here()
    if round_index == 0:
        line = z // 2 * 2 + y
        other_line = (1 - z // 2) * 2 + y
        return [(0, core, line), (0, core, other_line), (0, 1 - core, z)]
    swap = (z % 2 + z // 2 + y) % 2
    far = jnp.bitwise_xor(z, jnp.where(x == 0, 3 * swap, 1 + swap))
    return [(0, 0, z), (0, 1, far), (1, 0, far), (1, 1, z)]


def lists_kernel(round_index, rows_per, *refs):
    buckets = 1 if round_index == 0 else 2
    id_refs, (relations_ref, out_ref, *relate_ref) = refs[:buckets], refs[buckets:]
    blocks, _, slots = id_refs[0].shape
    pairs = blocks // 2
    lists = wanted_lists(round_index)
    if relate_ref:
        width = relations_ref.shape[1]
        full = -(-width // LANES) * LANES
        relations = jnp.pad(relations_ref[...].astype(F32), ((0, 0), (0, full - width)))
        relate_ref[0][...] = relations.T[:width].astype(BF16)
    lower = lax.broadcasted_iota(I32, (slots, slots), 0)
    upper = lax.broadcasted_iota(I32, (slots, slots), 1)
    before = (lower <= upper).astype(F32).astype(BF16)
    edge = lax.broadcasted_iota(I32, (1, slots), 1)
    one = jnp.ones_like(edge)
    order = [(n, pair) for n in range(len(lists)) for pair in range(pairs)]

    values, masks = [], []
    for ref in id_refs:
        packed = jnp.concatenate([ref[b, round_index : round_index + 1, :] for b in range(blocks)], 0)
        kinds = jnp.concatenate([ref[b, 2:3, :] for b in range(blocks)], 0)
        kinds = jnp.bitwise_and(jnp.right_shift(kinds, 16 * round_index), 65535)
        counts = jnp.sum(
            jnp.where(jnp.bitwise_and(packed, 65535) != DEAD, 1.0, 0.0), axis=1, keepdims=True
        )
        index = lax.broadcasted_iota(I32, (blocks, 1), 0)
        rank = jnp.zeros_like(index)
        for b in range(blocks):
            this = counts[b : b + 1]
            before_it = jnp.logical_or(
                this > counts, jnp.logical_and(this == counts, b < index)
            )
            rank = rank + jnp.where(before_it, 1, 0)
        row = jnp.where(rank < pairs, 2 * rank, 2 * (blocks - 1 - rank) + 1)

        def arranged(part, row=row):
            return jnp.concatenate(
                [
                    jnp.sum(jnp.where(row == b, part, 0), axis=0, keepdims=True)
                    for b in range(blocks)
                ],
                0,
            )

        packed, kinds = arranged(packed), arranged(kinds)
        sides = [jnp.bitwise_and(packed, 65535), jnp.right_shift(packed, 16)]
        values.append((sides, kinds))
    spots = []
    for bucket, side, group in lists:
        sides, kinds = values[bucket]
        if round_index == 0:
            ids = jnp.where(side == 0, sides[0], sides[1])
        else:
            ids = sides[side]
        live = sides[0] != DEAD
        holder = ids // rows_per
        local = jnp.where(live, ids - holder * rows_per, 0)
        if round_index == 0 and len(spots) < 2:
            mine = holder // 4 * 2 + holder % 2 == group
            which = holder // 2 % 2
        else:
            mine = holder // 2 == group
            which = holder % 2
        mine = jnp.logical_and(mine, live)
        spots.append((local, jnp.where(live, which, 0), mine, kinds))
        for k in range(2):
            masks.append(jnp.logical_and(mine, which == k).astype(F32))
    stacked = jnp.concatenate(masks, 0).astype(BF16)
    running = jnp.dot(stacked, before, preferred_element_type=F32)
    slots_of, late = [], []
    for n, (local, which, mine, kinds) in enumerate(spots):
        even, odd = (
            running[(2 * n + k) * blocks : (2 * n + k + 1) * blocks] for k in range(2)
        )
        second = lax.broadcasted_iota(I32, (blocks, 1), 0) % 2 == 1
        totals = [part[:, slots - 1 : slots] for part in (even, odd)]
        ahead = [
            jnp.concatenate([total[:1], total[:-1]], 0) for total in totals
        ]
        behind = [jnp.concatenate([total[1:], total[:1]], 0) for total in totals]
        whole = [
            total + jnp.where(second, a, b) for total, a, b in zip(totals, ahead, behind)
        ]
        even = even + jnp.where(second, ahead[0], 0.0)
        odd = odd + jnp.where(second, ahead[1], 0.0)
        room = CHUNK - whole[1]
        slot = jnp.where(
            which == 1, CHUNK - odd, jnp.where(even <= room, even - 1, CHUNK + even - 1 - room)
        )
        slots_of.append(jnp.where(mine, slot, -1.0))
        bit = lax.broadcasted_iota(I32, (blocks, 1), 0) // 2 + pairs * n
        over = jnp.logical_and(jnp.logical_not(second), whole[0] > room)
        late.append(jnp.where(over, jnp.left_shift(jnp.ones_like(bit), bit), 0))
    late = jnp.sum(jnp.concatenate(late, 0))
    chunk_ids = lax.broadcasted_iota(I32, (CHUNK, 2 * slots), 0).astype(F32)
    late_ids = lax.broadcasted_iota(I32, (LANES, 2 * slots), 0).astype(F32) + CHUNK
    edges = jnp.concatenate([edge, edge + slots], 1)
    nobody = jnp.full((1, LANES), NOBODY, I32)
    blank = jnp.zeros((1, LANES), I32)
    for n, (local, which, mine, kinds) in enumerate(spots):
        for pair in range(pairs):

            def joined(part, pair=pair):
                return jnp.concatenate([part[2 * pair : 2 * pair + 1], part[2 * pair + 1 : 2 * pair + 2]], 1)

            slot = joined(slots_of[n])
            columns = (
                jnp.concatenate(
                    [
                        joined(local),
                        joined(which),
                        joined(kinds),
                        edges // 32,
                        edges % 32,
                        jnp.ones_like(edges),
                    ]
                    + [jnp.zeros_like(edges)] * 2,
                    0,
                )
                .astype(F32)
                .astype(BF16)
            )

            def rows_at(slot_ids, slot=slot, columns=columns):
                chosen = (slot_ids == slot).astype(F32).astype(BF16)
                got = lax.dot_general(
                    columns, chosen, (((1,), (1,)), ((), ())), preferred_element_type=F32
                ).astype(I32)
                ids = jnp.where(got[5:6] > 0, got[1:2] * rows_per + got[0:1], NOBODY)
                return jnp.bitwise_or(ids, jnp.left_shift(got[3:4] * 32 + got[4:5], 16)), got[2:3]

            packed, kind = rows_at(chunk_ids)
            for k in range(2):
                cut = slice(k * LANES, (k + 1) * LANES)
                out_ref[n, pair, k : k + 1, :] = packed[:, cut]
                out_ref[n, pair, 3 + k : 4 + k, :] = kind[:, cut]
            out_ref[n, pair, 2:3, :] = nobody
            out_ref[n, pair, 5:6, :] = blank

            @pl.when(jnp.bitwise_and(jnp.right_shift(late, pairs * n + pair), 1) > 0)
            def _():
                packed, kind = rows_at(late_ids)
                out_ref[n, pair, 2:3, :] = packed
                out_ref[n, pair, 5:6, :] = kind


def make_lists(round_index, ids, relations, rows_per):
    width = relations.shape[1]

    def kernel(*refs):
        lists_kernel(round_index, rows_per, *refs)

    shapes = [jax.ShapeDtypeStruct((3 + round_index, ids[0].shape[0] // 2, 8, LANES), I32)]
    if round_index == 0:
        shapes.append(jax.ShapeDtypeStruct((width, relations.shape[0]), BF16))
    return pl.pallas_call(
        kernel,
        out_shape=tuple(shapes),
        in_specs=[VMEM] * (len(ids) + 1),
        out_specs=(VMEM,) * len(shapes),
        compiler_params=PARAMS,
        cost_estimate=pl.CostEstimate(
            flops=4_000_000_000, bytes_accessed=1_000_000, transcendentals=0
        ),
        name="make_lists",
    )(*ids, relations)


def both(left, right):
    return jnp.concatenate([left, right], 0)


def tile(source, target, relate, source_edge, target_edge):
    half = source.shape[0] // 2
    relate_re, relate_im = relate[:half], relate[half:]
    source = source.astype(F32)
    source_re, source_im = source[:half], source[half:]
    queries = both(
        source_re * relate_re - source_im * relate_im,
        source_re * relate_im + source_im * relate_re,
    ).astype(BF16)
    scores = lax.dot_general(
        queries, target, (((0,), (0,)), ((), ())), preferred_element_type=F32
    )
    edge_row = target_edge.astype(F32)
    edge_col = jnp.broadcast_to(source_edge.astype(F32), (8, source_edge.shape[1])).T[:, :1]
    bent = 0.5 * jnp.tanh(0.5 * scores)
    weights = jnp.where(
        edge_col == edge_row,
        bent - 0.5,
        jnp.where((edge_col < GROUP) == (edge_row < GROUP), (bent + 0.5) * (1.0 / GROUP), 0.0),
    ).astype(BF16)
    query_grad = lax.dot_general(
        target, weights, (((1,), (1,)), ((), ())), preferred_element_type=F32
    )
    target_grad = jnp.dot(queries, weights, preferred_element_type=F32).astype(BF16)
    grad_re, grad_im = query_grad[:half], query_grad[half:]
    source_grad = both(
        grad_re * relate_re + grad_im * relate_im,
        grad_im * relate_re - grad_re * relate_im,
    ).astype(BF16)
    return source_grad, target_grad


def tiles_kernel(round_index, *refs):
    lists, relations_ref, refs = refs[0], refs[1], refs[2:]
    count = 8 if round_index == 0 else 4
    table_refs, out_refs = refs[:count], refs[count : 2 * count]
    tables, picks, values, sums = refs[2 * count :]
    padded, rows = table_refs[0].shape
    total, pairs = lists.shape[:2]
    x, core, z, y = here()
    low = z % 2

    def choose(flag, first, second):
        return jnp.where(flag == 0, first, second)

    def lay(n, flag, first, second):
        tables[n, :, :rows] = choose(flag, first[...], second[...])
        tables[n, :, rows:] = choose(flag, second[...], first[...])

    if round_index == 0:
        near, far = table_refs[:4], table_refs[4:]

        @pl.when(core == 0)
        def _():
            lay(0, low, near[0], near[1])
            lay(1, low, near[2], near[3])
            lay(2, y, far[2], far[3])

        @pl.when(core == 1)
        def _():
            lay(0, low, far[0], far[1])
            lay(1, low, far[2], far[3])
            lay(2, y, near[0], near[1])
    else:
        for n, first in ((0, 0), (1, 2), (2, 2), (3, 0)):
            lay(n, y, table_refs[first], table_refs[first + 1])

    def packed_of(n, pair):
        return jnp.concatenate([lists[n, pair, k : k + 1, :] for k in range(2)], 1)

    def kinds_of(n, pair):
        return jnp.concatenate([lists[n, pair, 3 + k : 4 + k, :] for k in range(2)], 1)

    def one_hot(size, ids):
        row_ids = lax.broadcasted_iota(jnp.int16, (size, ids.shape[1]), 0)
        ids = jnp.where(jnp.logical_and(ids >= 0, ids < size), ids, -1).astype(jnp.int16)
        return jnp.where(row_ids == ids, jnp.ones((), BF16), jnp.zeros((), BF16))

    def relate_of(kinds):
        chosen = one_hot(relations_ref.shape[1], kinds)
        return jnp.dot(relations_ref[...], chosen, preferred_element_type=F32)

    span = pairs * LANES

    def side_ids(n, k):
        packed = [lists[n, pair, k : k + 1, :] for pair in range(pairs)]
        return jnp.bitwise_and(jnp.concatenate(packed, 1), 65535)

    lane = lax.broadcasted_iota(I32, (1, LANES), 1)
    notes = jnp.zeros((1, LANES), I32)
    for n in range(total):
        for pair in range(pairs):
            left, right, late = (
                jnp.bitwise_and(lists[n, pair, row : row + 1, :], 65535) for row in range(3)
            )
            over = jnp.logical_and(left >= rows, left < NOBODY)
            for bit, lane_at, there in (
                (2 * n, LANES - 1, over),
                (2 * n + 1, 0, right < rows),
                (8 + 4 * n + pair, 0, late < NOBODY),
            ):
                there = jnp.logical_and(there, lane == lane_at)
                notes = jnp.bitwise_or(notes, jnp.where(there, 1 << bit, 0))
    notes = jnp.sum(notes)
    crossed = [
        [jnp.bitwise_and(notes, 1 << (2 * n + k)) != 0 for k in range(2)] for n in range(total)
    ]
    for n in range(total):
        for k in range(2):
            pick = one_hot(rows, side_ids(n, k) - k * rows)
            picks[n, k] = pick
            values[n, :, k * span : (k + 1) * span] = jnp.dot(
                tables[n, :, k * rows : (k + 1) * rows], pick, preferred_element_type=F32
            ).astype(BF16)
    for n in range(total):
        for k in range(2):

            @pl.when(crossed[n][k])
            def _():
                pick = one_hot(rows, side_ids(n, k) - (1 - k) * rows)
                values[n, :, k * span : (k + 1) * span] += jnp.dot(
                    tables[n, :, (1 - k) * rows : (2 - k) * rows], pick, preferred_element_type=F32
                ).astype(BF16)

    def compute(pair, sources, targets):
        cuts = [slice(k * span + pair * LANES, k * span + (pair + 1) * LANES) for k in range(2)]

        def joined(chosen, get):
            return jnp.concatenate([get(n) for n in chosen], 1)

        def rows_of(chosen):
            return jnp.concatenate([values[n, :, cut] for n in chosen for cut in cuts], 1)

        def edges(chosen):
            return joined(chosen, lambda n: jnp.right_shift(packed_of(n, pair), 16))

        got = tile(
            rows_of(sources),
            rows_of(targets),
            relate_of(joined(sources, lambda n: kinds_of(n, pair))),
            edges(sources),
            edges(targets),
        )
        for chosen, grads in zip((sources, targets), got):
            for at, (n, cut) in enumerate((n, cut) for n in chosen for cut in cuts):
                values[n, :, cut] = grads[:, at * LANES : (at + 1) * LANES]

    if round_index == 0:

        @pl.when(core == 0)
        def _():
            for pair in range(pairs):
                compute(pair, (0, 1), (2,))

        @pl.when(core == 1)
        def _():
            for pair in range(pairs):
                compute(pair, (2,), (0, 1))
    else:
        for pair in range(pairs):
            compute(pair, (0,), (1,))
            compute(pair, (2,), (3,))

    def scatter(grads, pick):
        return lax.dot_general(grads, pick, (((1,), (1,)), ((), ())), preferred_element_type=F32)

    for n in range(total):
        for k in range(2):
            sums[n, :, k * rows : (k + 1) * rows] = scatter(
                values[n, :, k * span : (k + 1) * span], picks[n, k]
            )
    for n in range(total):
        for k in range(2):

            @pl.when(crossed[n][k])
            def _():
                pick = one_hot(rows, side_ids(n, k) - (1 - k) * rows)
                sums[n, :, (1 - k) * rows : (2 - k) * rows] += scatter(
                    values[n, :, k * span : (k + 1) * span], pick
                )

    @pl.when(jnp.right_shift(notes, 8) != 0)
    def _():
        spare = jnp.full((1, LANES), NOBODY, I32)

        def each(step, carry):
            pair, task = step // 2, step % 2
            if round_index == 0:
                chosen = (jnp.where(core == 0, task, 2), jnp.where(core == 0, 2, task))
            else:
                chosen = (2 * task, 2 * task + 1)
            has_late = [
                jnp.bitwise_and(jnp.right_shift(notes, 8 + 4 * chosen[side] + pair), 1)
                for side in range(2)
            ]

            def combine(combo, carry):
                late = (jnp.where(combo != 1, 1, 0), jnp.where(combo != 0, 1, 0))

                @pl.when(jnp.logical_and(has_late[0] >= late[0], has_late[1] >= late[1]))
                def _():
                    found = []
                    for side in range(2):

                        def rows_of(first, side=side):
                            left, right, extra = (
                                lists[chosen[side], pair, first + row : first + row + 1, :]
                                for row in range(3)
                            )
                            return jnp.where(
                                late[side] == 0,
                                jnp.concatenate([left, right], 1),
                                jnp.concatenate([extra, spare], 1),
                            )

                        packed = rows_of(0)
                        pick = one_hot(2 * rows, jnp.bitwise_and(packed, 65535))
                        gathered = jnp.dot(
                            tables[chosen[side]], pick, preferred_element_type=F32
                        ).astype(BF16)
                        found.append((gathered, pick, jnp.right_shift(packed, 16), rows_of))
                    grads = tile(
                        found[0][0],
                        found[1][0],
                        relate_of(found[0][3](3)),
                        found[0][2],
                        found[1][2],
                    )
                    for side in range(2):
                        sums[chosen[side]] += scatter(grads[side], found[side][1])

                return carry

            @pl.when(has_late[0] + has_late[1] > 0)
            def _():
                lax.fori_loop(0, 3, combine, 0)

            return carry

        lax.fori_loop(0, pairs * 2, each, 0)

    def part(total, which):
        return choose(which, total[:, :rows], total[:, rows:])

    if round_index > 0:
        near = sums[0] + sums[3]
        far = sums[1] + sums[2]
        out_refs[0][...] = part(near, y)
        out_refs[1][...] = part(near, 1 - y).astype(BF16)
        out_refs[2][...] = part(far, y).astype(BF16)
        out_refs[3][...] = part(far, 1 - y).astype(BF16)
        return

    def put(outs, n, which):
        for k in range(2):
            outs[k][...] = part(sums[n], which if k == 0 else 1 - which).astype(outs[k].dtype)

    def clear(outs):
        for ref in outs:
            ref[...] = jnp.zeros(ref.shape, ref.dtype)

    @pl.when(core == 0)
    def _():
        put(out_refs[0:2], 0, low)
        put(out_refs[2:4], 1, low)
        clear(out_refs[4:6])
        put(out_refs[6:8], 2, y)

    @pl.when(core == 1)
    def _():
        put(out_refs[0:2], 2, y)
        clear(out_refs[2:4])
        put(out_refs[4:6], 0, low)
        put(out_refs[6:8], 1, low)


def tiles(round_index, lists, relations, tables):
    padded, rows = tables[0].shape
    total, pairs = lists.shape[:2]

    def kernel(*refs):
        tiles_kernel(round_index, *refs)

    kinds = [F32] * 4 + [BF16] * 4 if round_index == 0 else [F32] + [BF16] * 3
    operands = (lists, relations, *tables)
    return pl.pallas_call(
        kernel,
        out_shape=tuple(jax.ShapeDtypeStruct((padded, rows), kind) for kind in kinds),
        in_specs=[VMEM] * len(operands),
        out_specs=(VMEM,) * len(kinds),
        scratch_shapes=[
            pltpu.VMEM((total, padded, 2 * rows), BF16),
            pltpu.VMEM((total, 2, rows, pairs * LANES), BF16),
            pltpu.VMEM((total, padded, pairs * CHUNK), BF16),
            pltpu.VMEM((total, padded, 2 * rows), F32),
        ],
        compiler_params=PARAMS,
        cost_estimate=pl.CostEstimate(
            flops=8_000_000_000, bytes_accessed=8_000_000, transcendentals=1_000_000
        ),
        name="tiles",
    )(*operands)


def update_kernel(master_ref, state_ref, own_ref, a_ref, b_ref, c_ref, *outs):
    gradient = (own_ref[...] + a_ref[...].astype(F32)) + (
        b_ref[...].astype(F32) + c_ref[...].astype(F32)
    )
    width = gradient.shape[0]
    state = state_ref[...] + jnp.sum(gradient * gradient, axis=0, keepdims=True) / width
    master = master_ref[...] - gradient * (learn_rate / jnp.sqrt(state))
    outs[0][...] = master
    outs[1][...] = state
    if len(outs) > 2:
        outs[2][...] = master.astype(BF16)


def update(master, state, own, a, b, c, last):
    shapes = [(master.shape, F32), (state.shape, F32)]
    if not last:
        shapes.append((master.shape, BF16))
    return pl.pallas_call(
        update_kernel,
        out_shape=tuple(jax.ShapeDtypeStruct(*shape) for shape in shapes),
        in_specs=[VMEM] * 6,
        out_specs=(VMEM,) * len(shapes),
        compiler_params=PARAMS,
        name="update",
    )(master, state, own, a, b, c)


def send(wire, routes):
    return [wire] + [move(wire, route) for route in routes]


def give_back(sums, routes):
    return [move(part, back(route)) for part, route in zip(sums, routes)]


def tile_body(entity_table, adagrad_state, relations, sources, targets, relation_ids, edge_counts):
    rows = entity_table.shape[1]
    entity = entity_table[0].T
    state = adagrad_state
    row_total = lax.axis_size("row")
    wire, ids = open_tables(entity, edge_counts, sources, targets, relation_ids, row_total)
    ids = lax.all_to_all(ids, "row", split_axis=0, concat_axis=0, tiled=True)
    near = [wire, None] + [move(wire, pairs) for pairs in FIRST[1:]]
    tied_wire, ids = lax.optimization_barrier((wire, ids))
    near[1] = move(tied_wire, FIRST[0])
    lists, relate = make_lists(0, [ids], relations, rows)
    other_ids = move(ids, SWAP_X)
    *near, lists = lax.optimization_barrier((*near, lists))
    far = [move(block, SWAP_CORE) for block in near]

    outs = tiles(0, lists, relate, near + far)
    outs, ids, other_ids = lax.optimization_barrier((outs, ids, other_ids))
    cross = [move(block, SWAP_CORE).astype(F32) for block in outs[4:]]
    sent = [(outs[1 + k] + cross[1 + k]).astype(BF16) for k in range(3)]
    parts = give_back(sent, FIRST)
    own, ids, other_ids, _ = lax.optimization_barrier((outs[0] + cross[0], ids, other_ids, sent))
    (lists,) = make_lists(1, [ids, other_ids], relations, rows)
    entity, lists = lax.optimization_barrier((entity, lists))
    entity, state, wire = update(entity, state, own, *parts, False)

    near = send(wire, SECOND)
    own, *parts = tiles(1, lists, relate, near)
    parts = give_back(parts, SECOND)
    entity, state = update(entity, state, own, *parts, True)
    return (entity.T[None], state)


def shifted(value, axis, steps):
    count = lax.axis_size(axis)
    pairs = [(source, (source + steps) % count) for source in range(count)]
    return lax.ppermute(value, axis, pairs)


def edge_grads(src_rows, dst_rows, rel_rows, live_mask):
    half_width = src_rows.shape[-1] // 2
    source = src_rows.astype(jnp.float32)
    relate = rel_rows.astype(jnp.float32)
    src_real = source[..., :half_width]
    src_imag = source[..., half_width:]
    rel_real = relate[..., :half_width]
    rel_imag = relate[..., half_width:]
    queries = jnp.concatenate(
        [src_real * rel_real - src_imag * rel_imag, src_real * rel_imag + src_imag * rel_real], -1
    ).astype(jnp.bfloat16)
    scores = jnp.einsum("bik,bjk->bij", queries, dst_rows, preferred_element_type=jnp.float32)
    block_size = scores.shape[-1]
    diagonal = jnp.arange(block_size)[:, None] == jnp.arange(block_size)[None, :]
    pair_mask = live_mask[:, :, None] * live_mask[:, None, :]
    weights = (
        jnp.where(diagonal, -jax.nn.sigmoid(-scores), jax.nn.sigmoid(scores) / block_size)
        * pair_mask
    ).astype(jnp.bfloat16)
    query_grad = jnp.einsum("bij,bjk->bik", weights, dst_rows, preferred_element_type=jnp.float32)
    dst_grad = jnp.einsum("bij,bik->bjk", weights, queries, preferred_element_type=jnp.float32)
    grad_real = query_grad[..., :half_width]
    grad_imag = query_grad[..., half_width:]
    src_grad = jnp.concatenate(
        [grad_real * rel_real + grad_imag * rel_imag, grad_imag * rel_real - grad_real * rel_imag],
        -1,
    )
    return (src_grad.astype(jnp.bfloat16), dst_grad.astype(jnp.bfloat16))


def slot_places(row_ids, rows_per, holders_total, capacity):
    holder = row_ids // rows_per
    onehot = (holder[:, None] == jnp.arange(holders_total)[None, :]).astype(jnp.int32)
    running = jnp.cumsum(onehot, axis=0)
    rank = jnp.sum(onehot * running, axis=-1) - 1
    place = holder * capacity + rank
    request = (
        jnp.zeros((holders_total * capacity,), jnp.int32).at[place].set(row_ids - holder * rows_per)
    )
    return (place, request.reshape(holders_total, capacity))


def plain_body(entity_table, adagrad_state, relations, sources, targets, relation_ids, edge_counts):
    entity = entity_table[0]
    adagrad = adagrad_state[0]
    rows_per = entity.shape[0]
    width = entity.shape[1]
    slot_total = sources.shape[-1]
    holders_total = lax.axis_size("row")
    capacity = 2 * slot_total // holders_total
    slot_ids = jnp.arange(slot_total)
    rel_columns = jnp.arange(relations.shape[0])
    for round_index in range(ROUNDS):
        shift_by = round_index + 1
        src_ids = sources[round_index, 0]
        dst_ids = targets[round_index, 0]
        live_total = edge_counts[round_index, 0, 0]
        live_mask = (slot_ids < live_total).astype(jnp.float32)
        rel_onehot = (relation_ids[round_index, 0][:, None] == rel_columns[None, :]).astype(
            jnp.bfloat16
        )
        rel_rows = jnp.dot(rel_onehot, relations, preferred_element_type=jnp.float32).astype(
            jnp.bfloat16
        )
        own_rows = entity.astype(jnp.bfloat16)
        src_place, src_request = slot_places(src_ids, rows_per, holders_total, capacity)
        dst_place, dst_request = slot_places(dst_ids, rows_per, holders_total, capacity)
        serve_table = shifted(own_rows, "dom", shift_by)
        wanted = (
            lax.all_to_all(src_request, "row", split_axis=0, concat_axis=0, tiled=True),
            lax.all_to_all(dst_request, "row", split_axis=0, concat_axis=0, tiled=True),
        )
        src_serve = jnp.take(own_rows, wanted[0].reshape(-1), axis=0).reshape(
            holders_total, capacity, width
        )
        dst_serve = jnp.take(serve_table, wanted[1].reshape(-1), axis=0).reshape(
            holders_total, capacity, width
        )
        answered = (
            lax.all_to_all(src_serve, "row", split_axis=0, concat_axis=0, tiled=True),
            lax.all_to_all(dst_serve, "row", split_axis=0, concat_axis=0, tiled=True),
        )
        dst_answer = answered[1]
        src_rows = jnp.take(answered[0].reshape(-1, width), src_place, axis=0)
        dst_rows = jnp.take(dst_answer.reshape(-1, width), dst_place, axis=0)
        src_grad, dst_grad = edge_grads(
            src_rows.reshape(-1, GROUP, width),
            dst_rows.reshape(-1, GROUP, width),
            rel_rows.reshape(-1, GROUP, width),
            live_mask.reshape(-1, GROUP),
        )
        src_grad = src_grad.reshape(slot_total, width)
        dst_grad = dst_grad.reshape(slot_total, width)
        blank = jnp.zeros((holders_total * capacity, width), jnp.bfloat16)
        src_buffer = blank.at[src_place].set(src_grad).reshape(holders_total, capacity, width)
        dst_buffer = blank.at[dst_place].set(dst_grad).reshape(holders_total, capacity, width)
        parts = (
            lax.all_to_all(src_buffer, "row", split_axis=0, concat_axis=0, tiled=True),
            lax.all_to_all(dst_buffer, "row", split_axis=0, concat_axis=0, tiled=True),
        )
        lhs_sum = jax.ops.segment_sum(
            parts[0].reshape(-1, width).astype(jnp.float32),
            wanted[0].reshape(-1),
            num_segments=rows_per,
        )
        other_sum = jax.ops.segment_sum(
            parts[1].reshape(-1, width).astype(jnp.float32),
            wanted[1].reshape(-1),
            num_segments=rows_per,
        )
        returned = shifted(other_sum, "dom", -shift_by)
        gradient = lhs_sum + returned
        adagrad = adagrad + jnp.mean(gradient * gradient, axis=-1)
        entity = entity - learn_rate * gradient / jnp.sqrt(adagrad)[:, None]
    return (entity[None], adagrad[None])


def solution(mesh):
    in_specs = (
        P("dom", "row", None),
        P("dom", "row"),
        P(),
        P(None, "dom", "row"),
        P(None, "dom", "row"),
        P(None, "dom", "row"),
        P(None, "dom", "row"),
    )
    out_specs = (P("dom", "row", None), P("dom", "row"))

    def body(entity_table, adagrad_state, relations, sources, *rest):
        fits = (
            (mesh.shape["dom"], mesh.shape["row"]) == (4, 8)
            and entity_table.shape[1] == 256
            and sources.shape[-1] == GROUP
        )
        chosen = tile_body if fits else plain_body
        return chosen(entity_table, adagrad_state, relations, sources, *rest)

    return jax.shard_map(body, mesh=mesh, in_specs=in_specs, out_specs=out_specs, check_vma=False)
```
